512 devices in a mesh: group: 8 (over y, core), cluster: 64 (over z, x).
Axes of the slice: x: 4, y: 4, z: 16, core: 2. Of those that a mesh axis runs over, the one named last changes fastest.
Arguments:
- queries: bfloat16 [57344, 4096], P(('group', 'cluster')), may hold values from -128 to 128
- cluster_id: int32 [57344, 1], P(('group', 'cluster')), may hold values from 0 to 63; in each aligned block of 112 rows (0 to 111, 112 to 223, ...) at most 4 rows name the same one
- block_list: int32 [57344, 2], P(('group', 'cluster')), may hold values from 0 to 2, all different within a row
- positive: int32 [57344], P(('group', 'cluster')), may hold values from 0 to 63
- passages: bfloat16 [98304, 4096], P(('group', 'cluster')), may hold values from -6 to 6
- pool_rows: bfloat16 [128, 4096], P('cluster'), may hold values from -5 to 5
- logit_scale: float32 [1], replicated, may hold values from 0.5 to 2
Outputs:
- query_grad: bfloat16 [57344, 4096], P(('group', 'cluster'))
- passage_grad: bfloat16 [98304, 4096], P(('group', 'cluster'))
- pool_grad: float32 [128, 4096], P('cluster')
- loss: float32 [1], replicated
- scale_grad: float32 [1], replicated
The draws below stay inside these ranges and needn't reach their ends.
Inputs may be any that keep to these rules, and one draw needn't show every extreme that they name: `cluster_id`: of the 112 queries of one device at most 4 name the same cluster, and in some device exactly 4 do; every cluster is named by some query. `block_list`: each row names 2 different blocks.
All inputs are finite; a program needn't handle non-finite values.
Results may differ from the reference program's by a relative error of at most 0.0095.
Values may be sent and summed in bfloat16 or wider, within the bound.
A program may use at most 64 MiB of HBM per device.

```python
import math
import jax
import jax.numpy as jnp
import numpy as np
from jax import lax

D = 4096
TQ = 112
BLOCK = 64
NB = 3
K = 2
TP = 192
CLUSTERS = 64
CAP = 4
POOL = 128
NQ = 57344
NP = 98304
N_GROUP = 8
N_CLUSTER = 64


def base_pool(key):
    return jnp.clip(jax.random.normal(jax.random.fold_in(key, 7), (POOL, D), jnp.float32), -5.0, 5.0)


def draw_pool_rows(key, part):
    return base_pool(key).astype(jnp.bfloat16)


def draw_queries(key, part):
    values_base = jnp.clip(jax.random.normal(jax.random.fold_in(key, 11), (NQ, D), jnp.float32), -5.0, 5.0)
    return values_base.astype(jnp.bfloat16)


def touch_ends(values, rng, least, high):
    longest = values.shape.index(max(values.shape))
    spots = []
    for shift in (0, 1):
        where = [jax.random.randint(jax.random.fold_in(rng, axis), (), 0, length) for axis, length in enumerate(values.shape)]
        where[longest] = (where[longest] + shift) % values.shape[longest]
        spots.append(tuple(where))
    return values.at[spots[0]].set(least).at[spots[1]].set(high)


def block_levels(rng, extent, pieces, low, largest):
    def one(position, parts):
        steps = jax.random.uniform(jax.random.fold_in(jax.random.fold_in(rng, 6), position), (parts,), jnp.float32, low / len(pieces), largest / len(pieces))
        return jnp.repeat(jnp.exp(steps), extent[position] // parts).reshape((-1,) + (1,) * (len(extent) - position - 1))

    level = one(*pieces[0])
    for cut in pieces[1:]:
        level = level * one(*cut)
    return level


def distinct(own_key, rows, number_of, top, lift):
    ranking = jax.random.permutation(jax.random.fold_in(own_key, 1), number_of)
    boost = ranking
    for power in range(3):
        boost = boost * boost // number_of
    boost = boost * lift // number_of
    lots = jax.random.randint(jax.random.fold_in(own_key, 2), (rows, number_of), 0, 4096) + boost
    sure = jax.random.permutation(jax.random.fold_in(own_key, 3), rows)[jnp.arange(number_of) % rows]
    lots = jnp.where(jnp.arange(rows)[:, None] == sure[None, :], 1 << 14, lots)
    priority = lots * number_of + jnp.arange(number_of)
    return lax.top_k(priority.astype(jnp.int32), top)[1].astype(jnp.int32)


def deal_out(own_key, own, number, rows, count, top, limit, skew):
    order = jax.random.permutation(own_key, count)
    packed, usual = portions_of(count, rows * top, limit, skew, True), portions_of(count, rows * top, limit, skew, False)
    places = jnp.arange(count)

    def named(tallies, rotation):
        used = int((tallies > 0).sum())
        fixed = max(1, used // 4)
        shifted = fixed + (places - fixed + rotation * (used - fixed)) % max(1, count - fixed)
        return jnp.zeros((count,), jnp.int32).at[order[jnp.where(places < fixed, places, shifted)]].set(jnp.asarray(tallies, jnp.int32))

    tallies = jnp.where(number % 4 == 0, named(packed, number // 4), named(usual, number - number // 4 - 1))
    mixed = jax.random.permutation(jax.random.fold_in(own, 3), count)
    donor, receiver = mixed[0:count // 2 * 2:2], mixed[1:count // 2 * 2:2]
    margin = jnp.minimum(tallies[donor] - 1, limit - tallies[receiver]) // 2
    margin = jnp.where((donor == order[0]) | (receiver == order[0]) | (tallies[receiver] == 0), 0, jnp.maximum(margin, 0))
    shifted = jax.random.randint(jax.random.fold_in(own, 4), (count // 2,), 0, 1 << 20) % (margin + 1)
    tallies = tallies.at[donor].add(-shifted).at[receiver].add(shifted)
    labels = jnp.searchsorted(jnp.cumsum(tallies), jnp.arange(rows * top), side="right").astype(jnp.int32)
    grid = labels.reshape(top, rows).T
    grid = grid[jax.random.permutation(jax.random.fold_in(own, 1), rows)]
    rotation = jax.random.randint(jax.random.fold_in(own, 2), (rows, 1), 0, top)
    return jnp.take_along_axis(grid, (jnp.arange(top)[None, :] + rotation) % top, axis=1)


def portions_of(amount, total, limit, slope, full):
    weights = [(1 << 20) // math.isqrt(grade ** slope) + 1 for grade in range(1, amount + 1)]
    largest = limit if full else min(limit, max(-(-total // amount), total * weights[0] // sum(weights)))
    least = 1 if total - largest >= amount - 1 else 0
    given, surplus = [largest] + [least] * (amount - 1), total - largest - least * (amount - 1)
    while surplus > 0:
        candidates = [i for i in range(1, amount) if given[i] < largest] or [i for i in range(1, amount) if given[i] < limit]
        mass, remaining = sum([weights[i] for i in candidates]), surplus
        for i in candidates:
            extra = min(limit - given[i], max(1, remaining * weights[i] // mass), surplus)
            given[i] = given[i] + extra
            surplus = surplus - extra
    return np.array(given)


def normal_values(stream_key, shape, scale, limit, cuts=(), kind=jnp.bfloat16):
    gain = block_levels(stream_key, shape, cuts, -0.22, 0.18) if cuts else 1.0
    drawn = jax.random.normal(stream_key, shape, jnp.float32) * scale * gain
    return jnp.minimum(jnp.maximum(drawn, -limit), limit).astype(kind)


def setup_inputs(seed: int = 0) -> dict:
    arg_keys = jax.random.split(jax.random.key(seed), 8)
    queries = draw_queries(jax.random.fold_in(arg_keys[7], 71), 0)
    cluster_id_keys = jax.random.split(jax.random.fold_in(arg_keys[1], 1), NQ // TQ)
    cluster_id_turns = jax.random.permutation(jax.random.fold_in(arg_keys[1], 3), NQ // TQ)
    cluster_id = jax.vmap(lambda own, number: deal_out(jax.random.fold_in(arg_keys[1], 2), own, number, TQ, CLUSTERS, 1, CAP, 2))(cluster_id_keys, cluster_id_turns).reshape((NQ, 1))
    block_list = distinct(arg_keys[2], NQ, NB, K, 0)
    positive = touch_ends(jax.random.randint(arg_keys[3], (NQ,), 0, BLOCK), jax.random.fold_in(arg_keys[3], 1), 0, BLOCK - 1).astype(jnp.int32)
    passages = normal_values(arg_keys[4], (NP, D), 1.0, 6.0, ((0, 512),))
    pool_rows = draw_pool_rows(jax.random.fold_in(arg_keys[7], 71), 0)
    logit_scale = jnp.clip(jnp.exp(jax.random.uniform(arg_keys[6], (1,), jnp.float32, math.log(0.5), math.log(2.0))), 0.5, 2.0)
    return {"queries": queries, "cluster_id": cluster_id, "block_list": block_list, "positive": positive, "passages": passages, "pool_rows": pool_rows, "logit_scale": logit_scale}


def owner_pass(routed, blocks, positive_col, live_rows, local_rows, pool_all, logit_scale):
    model_width = routed.shape[1]
    inv_root = 1.0 / math.sqrt(model_width)
    factor = logit_scale[0] * inv_root
    contract = (((1,), (1,)), ((), ()))
    raw_blk = lax.dot_general(routed, local_rows, contract, preferred_element_type=jnp.float32)
    raw_pool = lax.dot_general(routed, pool_all, contract, preferred_element_type=jnp.float32)
    score_blk = factor * raw_blk
    score_pool = factor * raw_pool
    block_count = local_rows.shape[0] // BLOCK
    block_ok = jnp.any(blocks[:, :, None] == jnp.arange(block_count, dtype=jnp.int32)[None, None, :], axis=1)
    allowed = jnp.repeat(block_ok, BLOCK, axis=1)
    peak_score = jnp.maximum(lax.optimization_barrier(jnp.max(jnp.where(allowed, score_blk, -jnp.inf), axis=1)), lax.optimization_barrier(jnp.max(score_pool, axis=1)))
    exp_blk = jnp.where(allowed, jnp.exp(score_blk - peak_score[:, None]), 0.0)
    exp_pool = jnp.exp(score_pool - peak_score[:, None])
    row_total = lax.optimization_barrier(jnp.sum(exp_blk, axis=1)) + lax.optimization_barrier(jnp.sum(exp_pool, axis=1))
    log_total = peak_score + jnp.log(row_total)
    target = blocks[:, 0] * BLOCK + positive_col
    target_hit = jnp.arange(local_rows.shape[0], dtype=jnp.int32)[None, :] == target[:, None]
    score_pos = lax.optimization_barrier(jnp.sum(jnp.where(target_hit, score_blk, 0.0), axis=1))
    weight = live_rows.astype(score_blk.dtype)
    loss_part = jnp.sum(weight * (log_total - score_pos))
    grad_blk = weight[:, None] * (exp_blk / row_total[:, None] - target_hit.astype(score_blk.dtype))
    grad_pool = weight[:, None] * (exp_pool / row_total[:, None])
    scale_part = inv_root * (jnp.sum(grad_blk * raw_blk) + jnp.sum(grad_pool * raw_pool))
    low_blk = grad_blk.astype(jnp.bfloat16)
    low_pool = grad_pool.astype(jnp.bfloat16)
    query_grad = (factor * (jnp.dot(low_blk, local_rows, preferred_element_type=jnp.float32) + jnp.dot(low_pool, pool_all, preferred_element_type=jnp.float32))).astype(jnp.bfloat16)
    passage_grad = (factor * lax.dot_general(low_blk, routed, (((0,), (0,)), ((), ())), preferred_element_type=jnp.float32)).astype(jnp.bfloat16)
    return (loss_part, scale_part, query_grad, passage_grad, low_pool, factor)

def reference(queries, cluster_id, block_list, positive, passages, pool_rows, logit_scale):
    query_total = queries.shape[0]
    owner_count = N_GROUP * N_CLUSTER
    rows_max = N_CLUSTER * CAP
    row_index = jnp.arange(query_total, dtype=jnp.int32)
    owner_of = (row_index // TQ // N_CLUSTER * N_CLUSTER + cluster_id[:, 0]).astype(jnp.int32)
    sorted_order = jnp.argsort(owner_of, stable=True).astype(jnp.int32)
    counts = lax.optimization_barrier(jnp.sum((owner_of[None, :] == jnp.arange(owner_count, dtype=jnp.int32)[:, None]).astype(jnp.int32), axis=1)).astype(jnp.int32)
    starts = (jnp.cumsum(counts) - counts).astype(jnp.int32)
    row_meta = jnp.concatenate([block_list, positive[:, None]], axis=1).astype(jnp.int32)
    sorted_rows = jnp.concatenate([queries[sorted_order], jnp.zeros((rows_max, D), jnp.bfloat16)], axis=0)
    sorted_meta = jnp.concatenate([row_meta[sorted_order], jnp.zeros((rows_max, K + 1), jnp.int32)], axis=0)
    sorted_index = jnp.concatenate([sorted_order, jnp.full((rows_max,), query_total, jnp.int32)], axis=0)

    def per_owner(state_now, owner_id):
        pool_sum, grads_all, loss_sum, scale_sum = state_now
        first_row = starts[owner_id]
        live_rows = jnp.arange(rows_max, dtype=jnp.int32) < counts[owner_id]
        routed = lax.dynamic_slice_in_dim(sorted_rows, first_row, rows_max, 0)
        routed = jnp.where(live_rows[:, None], routed, jnp.zeros_like(routed))
        meta_rows = lax.dynamic_slice_in_dim(sorted_meta, first_row, rows_max, 0)
        meta_rows = jnp.where(live_rows[:, None], meta_rows, jnp.zeros_like(meta_rows))
        local_rows = lax.dynamic_slice_in_dim(passages, (owner_id * TP).astype(jnp.int32), TP, 0)
        loss_part, scale_part, query_part, passage_part, low_pool, factor = owner_pass(routed, meta_rows[:, :K], meta_rows[:, K], live_rows, local_rows, pool_rows, logit_scale)
        pool_term = factor * lax.dot_general(low_pool, routed, (((0,), (0,)), ((), ())), preferred_element_type=jnp.float32)
        targets = lax.dynamic_slice_in_dim(sorted_index, first_row, rows_max, 0)
        targets = jnp.where(live_rows, targets, query_total).astype(jnp.int32)
        grads_all = grads_all.at[targets].set(query_part, mode='drop')
        return ((pool_sum + pool_term, grads_all, loss_sum + loss_part, scale_sum + scale_part), passage_part)
    start_state = (jnp.zeros((POOL, D), jnp.float32), jnp.zeros((query_total, D), jnp.bfloat16), jnp.zeros((), jnp.float32), jnp.zeros((), jnp.float32))
    final_state, passage_parts = lax.scan(per_owner, start_state, jnp.arange(owner_count, dtype=jnp.int32))
    pool_sum, grads_all, loss_sum, scale_sum = final_state
    passage_grad = passage_parts.reshape(NP, D)
    return (grads_all, passage_grad, pool_sum, (loss_sum / query_total).reshape(1), scale_sum.reshape(1))
```

```python
import math

import jax
import jax.numpy as jnp
from jax import lax
from jax.experimental import pallas as pl
from jax.experimental.pallas import tpu as pltpu
from jax.sharding import PartitionSpec as P

D = 4096
TQ = 112
BLOCK = 64
TP = 192
POOL = 128
NX = 4
NZ = 16
NY = 4
OWNERS = NX * NZ
CAP = 4
CHUNKS = 4
PER = OWNERS // CHUNKS
SLOTS = PER * CAP
W = D // 4
INV_ROOT = 1.0 / math.sqrt(D)
MESH = pl.DeviceIdType.MESH
F32 = jnp.float32
BF16 = jnp.bfloat16


def iota(shape, axis):
    return lax.broadcasted_iota(jnp.int32, shape, axis)


def onehot(mask):
    return jnp.where(mask, 1.0, 0.0).astype(BF16)


def kernel(
    q_ref, cl_ref, bl_ref, pos_ref, p_ref, piece_ref, scale_ref,
    home_ref, pg_ref, poolg_ref, loss_ref, sgrad_ref,
    snd, rcv, msnd, mrcv, gsnd, grcv, stack, routed, low, lowt, acc, gp, pool,
    pt, rc, s1, ry, s2, rx, zb, rz, fin, gb, sc, rcs, rys, rxs,
    d_send, d_recv, m_send, m_recv, g_send, g_recv, p_send, p_recv, r_send, r_recv, t_send, t_recv,
):
    grp = lax.axis_index("group")
    clu = lax.axis_index("cluster")
    y, core = grp // 2, grp % 2
    z, x = clu // NX, clu % NX

    def cluster_peer(dz, dx):
        return (grp, ((z + dz + NZ) % NZ) * NX + (x + dx + NX) % NX)

    def group_peer(py, pc):
        return (py * 2 + pc, clu)

    def offset(o):
        return ((o // 4) % 4) * 4 + o // 16, o % 4

    def copy(src, dst, send, recv, peer):
        return pltpu.make_async_remote_copy(
            src_ref=src, dst_ref=dst, send_sem=send, recv_sem=recv, device_id=peer, device_id_type=MESH
        )

    here = (grp, clu)
    barrier = pltpu.get_barrier_semaphore()

    def greet(o, carry):
        dz, dx = offset(o)
        pl.semaphore_signal(barrier, inc=1, device_id=cluster_peer(dz, dx), device_id_type=MESH)
        return carry

    lax.fori_loop(1, OWNERS, greet, 0)

    def greet_group(k, carry):
        pl.semaphore_signal(barrier, inc=1, device_id=((grp + k) % 8, clu), device_id_type=MESH)
        return carry

    lax.fori_loop(1, 8, greet_group, 0)

    factor = scale_ref[0] * INV_ROOT

    a_iota, b_iota = iota((TQ, TQ), 0), iota((TQ, TQ), 1)
    eye = a_iota == b_iota

    def to_col(row):
        return jnp.sum(jnp.where(eye, row.astype(F32), 0.0), axis=1, keepdims=True)

    cl_row = cl_ref[...]
    cl_col = to_col(cl_row).astype(jnp.int32)
    same = cl_col == cl_row
    rank_row = jnp.sum(jnp.where(same & (a_iota < b_iota), 1.0, 0.0), axis=0, keepdims=True).astype(jnp.int32)
    rank_col = jnp.sum(jnp.where(same & (b_iota < a_iota), 1.0, 0.0), axis=1, keepdims=True).astype(jnp.int32)

    def offset_of(cl):
        dz = ((cl >> 2) - z) & 15
        return (dz & 3) * 16 + (dz >> 2) * 4 + ((cl - x) & 3)

    off_row, off_col = offset_of(cl_row), offset_of(cl_col)
    place_row = off_row * 16 + rank_row
    place_col = off_col * 16 + rank_col

    lane = iota((TQ, 128), 1)
    field = lane >> 2
    block0, block1, position = to_col(bl_ref[0:1, :]), to_col(bl_ref[1:2, :]), to_col(pos_ref[...])
    value = jnp.where(field == 0, block0, jnp.where(field == 1, block1, jnp.where(field == 2, position, 1.0)))
    value = jnp.where((rank_col == (lane & 3)) & (field < 4), value, 0.0).astype(BF16)
    meta = jnp.dot(onehot(iota((OWNERS, TQ), 0) == off_row), value, preferred_element_type=F32)
    msnd[:, 0, :] = meta

    def build(c, carry):
        row = iota((PER * 16, TQ), 0) + c * (PER * 16)
        total = jnp.zeros((PER * 16, W), F32)
        for b in range(4):
            pick = onehot(row == place_row + 4 * b)
            total = total + jnp.dot(pick, q_ref[:, b * W:(b + 1) * W], preferred_element_type=F32)
        snd[pl.ds(c * PER, PER)] = total.astype(BF16).reshape(PER, 16, W)
        return carry

    def send_chunk(c):
        def step(o, carry):
            dz, dx = offset(o)
            peer = cluster_peer(dz, dx)
            copy(msnd.at[o], mrcv.at[o], m_send, m_recv.at[o // PER], peer).start()
            copy(snd.at[o], rcv.at[o], d_send, d_recv.at[o // PER], peer).start()
            return carry

        lax.fori_loop(1 if c == 0 else c * PER, (c + 1) * PER, step, 0)

    build(0, 0)
    gp[y, x, z] = piece_ref[y]
    pl.semaphore_wait(barrier, OWNERS - 1 + 7)

    def pool_z(k, carry):
        copy(gp.at[y, x, z], gp.at[y, x, z], p_send.at[0], p_recv.at[0], cluster_peer(k, 0)).start()
        return carry

    lax.fori_loop(1, NZ, pool_z, 0)
    for c in range(CHUNKS):
        send_chunk(c)
        if c + 1 < CHUNKS:
            build(c + 1, 0)
    rcv[0] = snd[0]
    mrcv[0] = msnd[0]

    some = gp.at[y, x, pl.ds(0, NZ - 1)]
    copy(some, some, p_send.at[0], p_recv.at[0], here).wait()
    for k in range(1, NX):
        copy(gp.at[y, x], gp.at[y, x], p_send.at[1], p_recv.at[1], cluster_peer(0, k)).start()
    some = gp.at[y, pl.ds(0, NX - 1)]
    copy(some, some, p_send.at[1], p_recv.at[1], here).wait()
    for k in range(1, NY):
        copy(gp.at[y], gp.at[y], p_send.at[2], p_recv.at[2], group_peer((y + k) % NY, core)).start()
    some = gp.at[pl.ds(0, NY - 1)]
    copy(some, some, p_send.at[2], p_recv.at[2], here).wait()

    def spread(yy, carry):
        flat = gp[yy].reshape(OWNERS * 16, 128)
        i, j = iota((POOL, OWNERS * 16), 0), iota((POOL, OWNERS * 16), 1)
        base = (i >> 5) * (NZ * 16) + (i & 15) * 16 + ((i >> 4) & 1) * 8
        for cb in range(8):
            part = jnp.dot(onehot(j == base + cb), flat, preferred_element_type=F32).astype(BF16)
            pool[:, pl.ds(pl.multiple_of(yy * W + cb * 128, 128), 128)] = part
        return carry

    lax.fori_loop(0, NY, spread, 0)

    i, j = iota((256, 256), 0), iota((256, 256), 1)
    unmix = onehot(((i >> 2) & 15) * 16 + (i >> 6) * 4 + (i & 3) == j)
    mix = onehot(((j >> 2) & 15) * 16 + (j >> 6) * 4 + (j & 3) == i)
    contract = (((1,), (1,)), ((), ()))

    def work(c, carry):
        loss_sum, scale_sum = carry
        some = rcv.at[pl.ds(c * PER, PER)]
        rows = rcv[pl.ds(c * PER, PER)].reshape(PER * 16, W)
        plain = jnp.dot(unmix, rows, preferred_element_type=F32).astype(BF16)
        for b in range(4):
            routed[pl.ds(c * SLOTS, SLOTS), b * W:(b + 1) * W] = plain[b * SLOTS:(b + 1) * SLOTS]
        mine = routed[pl.ds(c * SLOTS, SLOTS), :]
        raw_blk = lax.dot_general(mine, p_ref[...], contract, preferred_element_type=F32)
        raw_pool = lax.dot_general(mine, pool[...], contract, preferred_element_type=F32)
        expand = onehot((iota((SLOTS, PER), 0) >> 2) == iota((SLOTS, PER), 1))
        got = mrcv[pl.ds(c * PER, PER), 0, :].astype(BF16)
        got = jnp.dot(expand, got, preferred_element_type=F32)
        lanes, rank = iota((SLOTS, 128), 1), iota((SLOTS, 128), 0) & 3

        def column(f):
            return jnp.sum(jnp.where(lanes == 4 * f + rank, got, 0.0), axis=1, keepdims=True)

        first, second, place, weight = column(0), column(1), column(2), column(3)
        cand = iota((SLOTS, TP), 1)
        block = (cand >> 6).astype(F32)
        allowed = (block == first) | (block == second)
        hit = cand.astype(F32) == first * BLOCK + place
        score_blk = factor * raw_blk
        score_pool = factor * raw_pool
        peak = jnp.maximum(
            jnp.max(jnp.where(allowed, score_blk, -jnp.inf), axis=1, keepdims=True),
            jnp.max(score_pool, axis=1, keepdims=True),
        )
        exp_blk = jnp.where(allowed, jnp.exp(jnp.where(allowed, score_blk - peak, 0.0)), 0.0)
        exp_pool = jnp.exp(score_pool - peak)
        total = jnp.sum(exp_blk, axis=1, keepdims=True) + jnp.sum(exp_pool, axis=1, keepdims=True)
        log_total = peak + jnp.log(total)
        score_pos = jnp.sum(jnp.where(hit, score_blk, 0.0), axis=1, keepdims=True)
        loss_sum = loss_sum + jnp.sum(weight * (log_total - score_pos), axis=0, keepdims=True)
        grad_blk = weight * (exp_blk / total - jnp.where(hit, 1.0, 0.0))
        grad_pool = weight * (exp_pool / total)
        both = jnp.sum(grad_blk * raw_blk, axis=1, keepdims=True) + jnp.sum(grad_pool * raw_pool, axis=1, keepdims=True)
        scale_sum = scale_sum + INV_ROOT * jnp.sum(both, axis=0, keepdims=True)
        low[pl.ds(c * SLOTS, SLOTS), 0:TP] = grad_blk
        low[pl.ds(c * SLOTS, SLOTS), 256:256 + POOL] = grad_pool
        low_blk, low_pool = grad_blk.astype(BF16), grad_pool.astype(BF16)
        for b in range(4):
            cols = slice(b * W, (b + 1) * W)
            part = jnp.dot(low_blk, p_ref[:, cols], preferred_element_type=F32)
            part = part + jnp.dot(low_pool, pool[:, cols], preferred_element_type=F32)
            stack[b * SLOTS:(b + 1) * SLOTS, :] = (factor * part).astype(BF16)
        mixed = jnp.dot(mix, stack[...], preferred_element_type=F32).astype(BF16)
        gsnd[pl.ds(c * PER, PER)] = mixed.reshape(PER, 16, W)
        return loss_sum, scale_sum

    def bundles(ref, c):
        lo = 1 if c == 0 else c * PER
        return ref.at[pl.ds(lo, (c + 1) * PER - lo)]

    def owner_step(c, sums):
        some = bundles(rcv, c)
        copy(some, some, d_send, d_recv.at[c], here).wait_recv()
        some = bundles(mrcv, c)
        copy(some, some, m_send, m_recv.at[c], here).wait_recv()
        sums = work(c, sums)

        def back(o, carry):
            dz, dx = offset(o)
            copy(gsnd.at[o], grcv.at[o], g_send, g_recv.at[o // PER], cluster_peer(-dz, -dx)).start()
            return carry

        lax.fori_loop(1 if c == 0 else c * PER, (c + 1) * PER, back, 0)
        return sums

    sums = (jnp.zeros((1, 1), F32), jnp.zeros((1, 1), F32))
    for c in range(CHUNKS):
        sums = owner_step(c, sums)
    grcv[0] = gsnd[0]

    low[:, TP:256] = jnp.zeros((256, 256 - TP), F32)
    lowt[...] = low[...].T.astype(BF16)

    def pool_term(k, carry):
        cols = pl.ds(pl.multiple_of(k * 512, 512), 512)
        part = jnp.dot(lowt[256:256 + POOL, :], routed[:, cols], preferred_element_type=F32)
        pt[k % 2, k // 2] = factor * part
        return carry

    lax.fori_loop(0, 8, pool_term, 0)
    tile_lane = iota((8, 128), 1)
    sc[0] = jnp.where(tile_lane == 0, sums[0], jnp.where(tile_lane == 1, sums[1], 0.0))

    peer = group_peer(y, 1 - core)
    move = [
        copy(pt.at[1 - core], rc, r_send.at[0], r_recv.at[0], peer),
        copy(sc.at[0], rcs, t_send.at[0], t_recv.at[0], peer),
    ]
    for one in move:
        one.start()

    def passage_term(k, carry):
        cols = pl.ds(pl.multiple_of(k * 512, 512), 512)
        part = jnp.dot(lowt[0:TP, :], routed[:, cols], preferred_element_type=F32)
        pg_ref[:, cols] = (factor * part).astype(BF16)
        return carry

    lax.fori_loop(0, 8, passage_term, 0)
    for one in move:
        one.wait()
    s1[...] = pt[core] + rc[...]
    sc[1] = sc[0] + rcs[...]

    for k in range(1, NY):
        to = (y + k) % NY
        copy(s1.at[to], ry.at[k - 1], r_send.at[1], r_recv.at[1], group_peer(to, core)).start()
        copy(sc.at[1], rys.at[k - 1], t_send.at[1], t_recv.at[1], group_peer(to, core)).start()
    copy(ry, ry, r_send.at[1], r_recv.at[1], here).wait()
    copy(rys, rys, t_send.at[1], t_recv.at[1], here).wait()
    s2[...] = (s1[y] + ry[0] + ry[1] + ry[2]).reshape(NX, 32, 512)
    sc[2] = sc[1] + rys[0] + rys[1] + rys[2]

    for k in range(1, NX):
        to = (x + k) % NX
        copy(s2.at[to], rx.at[k - 1], r_send.at[2], r_recv.at[2], cluster_peer(0, k)).start()
        copy(sc.at[2], rxs.at[k - 1], t_send.at[2], t_recv.at[2], cluster_peer(0, k)).start()
    copy(rx, rx, r_send.at[2], r_recv.at[2], here).wait()
    copy(rxs, rxs, t_send.at[2], t_recv.at[2], here).wait()
    s3 = s2[x] + rx[0] + rx[1] + rx[2]
    scalars = sc[2] + rxs[0] + rxs[1] + rxs[2]
    for r in range(2):
        for cb in range(4):
            zb[:, r * 4 + cb, :] = s3[r * NZ:(r + 1) * NZ, cb * 128:(cb + 1) * 128]
    zb[:, 8:16, :] = jnp.broadcast_to(scalars[None], (NZ, 8, 128))

    def to_z(k, carry):
        copy(zb.at[(z + k) % NZ], rz.at[k - 1], r_send.at[3], r_recv.at[3], cluster_peer(k, 0)).start()
        return carry

    lax.fori_loop(1, NZ, to_z, 0)
    copy(rz, rz, r_send.at[3], r_recv.at[3], here).wait()
    last = zb[z] + jnp.sum(rz[...], axis=0)
    fin[...] = last[0:8]
    gb[grp] = last[0:8]
    loss_ref[0] = jnp.sum(jnp.where(tile_lane[0:1] == 0, last[8:9], 0.0)) * (1.0 / (TQ * OWNERS * 8))
    sgrad_ref[0] = jnp.sum(jnp.where(tile_lane[0:1] == 1, last[8:9], 0.0))

    def to_group(k, carry):
        copy(fin, gb.at[grp], r_send.at[4], r_recv.at[4], ((grp + k) % 8, clu)).start()
        return carry

    lax.fori_loop(1, 8, to_group, 0)

    def take(c):
        some = bundles(grcv, c)
        copy(some, some, g_send, g_recv.at[c], here).wait_recv()
        rows = grcv[pl.ds(c * PER, PER)].reshape(PER * 16, W)
        lanes = iota((TQ, PER * 16), 1) + c * (PER * 16)
        for b in range(4):
            part = jnp.dot(onehot(lanes == place_col + 4 * b), rows, preferred_element_type=F32)
            if c == 0:
                acc[:, b * W:(b + 1) * W] = part
            elif c + 1 < CHUNKS:
                acc[:, b * W:(b + 1) * W] += part
            else:
                home_ref[:, b * W:(b + 1) * W] = (acc[:, b * W:(b + 1) * W] + part).astype(BF16)

    for c in range(CHUNKS):
        take(c)

    some = gb.at[pl.ds(0, 7)]
    copy(some, some, r_send.at[4], r_recv.at[4], here).wait()
    for g in range(8):
        for r in range(2):
            for cb in range(4):
                col = g * 512 + cb * 128
                poolg_ref[r:r + 1, col:col + 128] = gb[g, r * 4 + cb:r * 4 + cb + 1, :]

    some = rcv.at[pl.ds(1, OWNERS - 1)]
    copy(some, some, d_send, d_recv.at[0], here).wait_send()
    copy(some, some, g_send, g_recv.at[0], here).wait_send()
    some = mrcv.at[pl.ds(1, OWNERS - 1)]
    copy(some, some, m_send, m_recv.at[0], here).wait_send()


def per_device(queries, cluster_id, block_list, positive, passages, pool_rows, logit_scale):
    piece = pool_rows.reshape(2, 4, 8, 128).transpose(1, 0, 2, 3).reshape(4, 16, 128)
    vm = pl.BlockSpec(memory_space=pltpu.VMEM)
    sm = pl.BlockSpec(memory_space=pltpu.SMEM)
    bundle = pltpu.VMEM((OWNERS, 16, W), BF16)
    note = pltpu.VMEM((OWNERS, 1, 128), F32)
    dma = pltpu.SemaphoreType.DMA
    home, passage_grad, pool_grad, loss, scale_grad = pl.pallas_call(
        kernel,
        out_shape=(
            jax.ShapeDtypeStruct((TQ, D), BF16),
            jax.ShapeDtypeStruct((TP, D), BF16),
            jax.ShapeDtypeStruct((2, D), F32),
            jax.ShapeDtypeStruct((1,), F32),
            jax.ShapeDtypeStruct((1,), F32),
        ),
        in_specs=[vm] * 6 + [sm],
        out_specs=(vm, vm, vm, sm, sm),
        scratch_shapes=[
            bundle, bundle, note, note, bundle, bundle,
            pltpu.VMEM((256, W), BF16),
            pltpu.VMEM((256, D), BF16),
            pltpu.VMEM((256, 384), F32),
            pltpu.VMEM((384, 256), BF16),
            pltpu.VMEM((TQ, D), F32),
            pltpu.VMEM((NY, NX, NZ, 16, 128), BF16),
            pltpu.VMEM((POOL, D), BF16),
            pltpu.VMEM((2, NY, POOL, 512), F32),
            pltpu.VMEM((NY, POOL, 512), F32),
            pltpu.VMEM((NY, POOL, 512), F32),
            pltpu.VMEM((NY - 1, POOL, 512), F32),
            pltpu.VMEM((NX, 32, 512), F32),
            pltpu.VMEM((NX - 1, 32, 512), F32),
            pltpu.VMEM((NZ, 16, 128), F32),
            pltpu.VMEM((NZ - 1, 16, 128), F32),
            pltpu.VMEM((8, 128), F32),
            pltpu.VMEM((8, 8, 128), F32),
            pltpu.VMEM((3, 8, 128), F32),
            pltpu.VMEM((8, 128), F32),
            pltpu.VMEM((NY - 1, 8, 128), F32),
            pltpu.VMEM((NX - 1, 8, 128), F32),
            dma, dma((CHUNKS,)), dma, dma((CHUNKS,)), dma, dma((CHUNKS,)),
            dma((3,)), dma((3,)), dma((5,)), dma((5,)), dma((3,)), dma((3,)),
        ],
        compiler_params=pltpu.CompilerParams(
            collective_id=0, has_side_effects=True, vmem_limit_bytes=48 * 1024 * 1024
        ),
        cost_estimate=pl.CostEstimate(flops=4 * 10**9, bytes_accessed=6 * 10**6, transcendentals=82000),
    )(
        queries,
        cluster_id.reshape(1, TQ),
        block_list.T,
        positive.reshape(1, TQ),
        passages,
        piece,
        logit_scale,
    )
    return home, passage_grad, pool_grad, loss, scale_grad


def solution(mesh):
    placed = (
        P(("group", "cluster"), None),
        P(("group", "cluster"), None),
        P(("group", "cluster"), None),
        P(("group", "cluster")),
        P(("group", "cluster"), None),
        P("cluster", None),
        P(),
    )
    return jax.shard_map(
        per_device,
        mesh=mesh,
        in_specs=placed,
        out_specs=(
            P(("group", "cluster"), None),
            P(("group", "cluster"), None),
            P("cluster", None),
            P(),
            P(),
        ),
        check_vma=False,
    )
```

```python
import math

import jax
import jax.numpy as jnp
from jax import lax
from jax.experimental import pallas as pl
from jax.experimental.pallas import tpu as pltpu
from jax.sharding import PartitionSpec as P

D = 4096
TQ = 112
BLOCK = 64
TP = 192
POOL = 128
NX = 4
NZ = 16
NY = 4
OWNERS = NX * NZ
CAP = 4
CHUNKS = 4
PER = OWNERS // CHUNKS
SLOTS = PER * CAP
W = D // 4
INV_ROOT = 1.0 / math.sqrt(D)
MESH = pl.DeviceIdType.MESH
F32 = jnp.float32
BF16 = jnp.bfloat16


def iota(shape, axis):
    return lax.broadcasted_iota(jnp.int32, shape, axis)


def onehot(mask):
    return jnp.where(mask, 1.0, 0.0).astype(BF16)


def full_kernel(
    q_ref, cl_ref, bl_ref, pos_ref, p_ref, piece_ref, scale_ref,
    home_ref, pg_ref, poolg_ref, loss_ref, sgrad_ref,
    snd, rcv, msnd, mrcv, gsnd, grcv, stack, routed, low, lowt, acc, gp, pool,
    pt, rc, s1, ry, s2, rx, zb, rz, fin, gb, sc, rcs, rys, rxs,
    d_send, d_recv, m_send, m_recv, g_send, g_recv, p_send, p_recv, r_send, r_recv, t_send, t_recv,
):
    grp = lax.axis_index("group")
    clu = lax.axis_index("cluster")
    y, core = grp // 2, grp % 2
    z, x = clu // NX, clu % NX

    def cluster_peer(dz, dx):
        return (grp, ((z + dz + NZ) % NZ) * NX + (x + dx + NX) % NX)

    def group_peer(py, pc):
        return (py * 2 + pc, clu)

    def offset(o):
        return ((o // 4) % 4) * 4 + o // 16, o % 4

    def copy(src, dst, send, recv, peer):
        return pltpu.make_async_remote_copy(
            src_ref=src, dst_ref=dst, send_sem=send, recv_sem=recv, device_id=peer, device_id_type=MESH
        )

    here = (grp, clu)
    barrier = pltpu.get_barrier_semaphore()

    def greet(o, carry):
        dz, dx = offset(o)
        pl.semaphore_signal(barrier, inc=1, device_id=cluster_peer(dz, dx), device_id_type=MESH)
        return carry

    lax.fori_loop(1, OWNERS, greet, 0)

    def greet_group(k, carry):
        pl.semaphore_signal(barrier, inc=1, device_id=((grp + k) % 8, clu), device_id_type=MESH)
        return carry

    lax.fori_loop(1, 8, greet_group, 0)

    factor = scale_ref[0] * INV_ROOT

    a_iota, b_iota = iota((TQ, TQ), 0), iota((TQ, TQ), 1)
    eye = a_iota == b_iota

    def to_col(row):
        return jnp.sum(jnp.where(eye, row.astype(F32), 0.0), axis=1, keepdims=True)

    cl_row = cl_ref[...]
    cl_col = to_col(cl_row).astype(jnp.int32)
    same = cl_col == cl_row
    rank_row = jnp.sum(jnp.where(same & (a_iota < b_iota), 1.0, 0.0), axis=0, keepdims=True).astype(jnp.int32)
    rank_col = jnp.sum(jnp.where(same & (b_iota < a_iota), 1.0, 0.0), axis=1, keepdims=True).astype(jnp.int32)

    def offset_of(cl):
        dz = ((cl >> 2) - z) & 15
        return (dz & 3) * 16 + (dz >> 2) * 4 + ((cl - x) & 3)

    off_row, off_col = offset_of(cl_row), offset_of(cl_col)
    place_row = off_row * 16 + rank_row
    place_col = off_col * 16 + rank_col

    lane = iota((TQ, 128), 1)
    field = lane >> 2
    block0, block1, position = to_col(bl_ref[0:1, :]), to_col(bl_ref[1:2, :]), to_col(pos_ref[...])
    value = jnp.where(field == 0, block0, jnp.where(field == 1, block1, jnp.where(field == 2, position, 1.0)))
    value = jnp.where((rank_col == (lane & 3)) & (field < 4), value, 0.0).astype(BF16)
    meta = jnp.dot(onehot(iota((OWNERS, TQ), 0) == off_row), value, preferred_element_type=F32)
    msnd[:, 0, :] = meta

    def build(c, carry):
        row = iota((PER * 16, TQ), 0) + c * (PER * 16)
        total = jnp.zeros((PER * 16, W), F32)
        for b in range(4):
            pick = onehot(row == place_row + 4 * b)
            total = total + jnp.dot(pick, q_ref[:, b * W:(b + 1) * W], preferred_element_type=F32)
        snd[pl.ds(c * PER, PER)] = total.astype(BF16).reshape(PER, 16, W)
        return carry

    def send_chunk(c):
        def step(o, carry):
            dz, dx = offset(o)
            peer = cluster_peer(dz, dx)
            copy(msnd.at[o], mrcv.at[o], m_send, m_recv.at[o // PER], peer).start()
            copy(snd.at[o], rcv.at[o], d_send, d_recv.at[o // PER], peer).start()
            return carry

        lax.fori_loop(1 if c == 0 else c * PER, (c + 1) * PER, step, 0)

    build(0, 0)
    gp[y, x, z] = piece_ref[y]
    pl.semaphore_wait(barrier, OWNERS - 1 + 7)

    def pool_z(k, carry):
        copy(gp.at[y, x, z], gp.at[y, x, z], p_send.at[0], p_recv.at[0], cluster_peer(k, 0)).start()
        return carry

    lax.fori_loop(1, NZ, pool_z, 0)
    for c in range(CHUNKS):
        send_chunk(c)
        if c + 1 < CHUNKS:
            build(c + 1, 0)
    rcv[0] = snd[0]
    mrcv[0] = msnd[0]

    some = gp.at[y, x, pl.ds(0, NZ - 1)]
    copy(some, some, p_send.at[0], p_recv.at[0], here).wait()
    for k in range(1, NX):
        copy(gp.at[y, x], gp.at[y, x], p_send.at[1], p_recv.at[1], cluster_peer(0, k)).start()
    some = gp.at[y, pl.ds(0, NX - 1)]
    copy(some, some, p_send.at[1], p_recv.at[1], here).wait()
    for k in range(1, NY):
        copy(gp.at[y], gp.at[y], p_send.at[2], p_recv.at[2], group_peer((y + k) % NY, core)).start()
    some = gp.at[pl.ds(0, NY - 1)]
    copy(some, some, p_send.at[2], p_recv.at[2], here).wait()

    def spread(yy, carry):
        flat = gp[yy].reshape(OWNERS * 16, 128)
        i, j = iota((POOL, OWNERS * 16), 0), iota((POOL, OWNERS * 16), 1)
        base = (i >> 5) * (NZ * 16) + (i & 15) * 16 + ((i >> 4) & 1) * 8
        for cb in range(8):
            part = jnp.dot(onehot(j == base + cb), flat, preferred_element_type=F32).astype(BF16)
            pool[:, pl.ds(pl.multiple_of(yy * W + cb * 128, 128), 128)] = part
        return carry

    lax.fori_loop(0, NY, spread, 0)

    i, j = iota((256, 256), 0), iota((256, 256), 1)
    unmix = onehot(((i >> 2) & 15) * 16 + (i >> 6) * 4 + (i & 3) == j)
    mix = onehot(((j >> 2) & 15) * 16 + (j >> 6) * 4 + (j & 3) == i)
    contract = (((1,), (1,)), ((), ()))

    def work(c, carry):
        loss_sum, scale_sum = carry
        some = rcv.at[pl.ds(c * PER, PER)]
        rows = rcv[pl.ds(c * PER, PER)].reshape(PER * 16, W)
        plain = jnp.dot(unmix, rows, preferred_element_type=F32).astype(BF16)
        for b in range(4):
            routed[pl.ds(c * SLOTS, SLOTS), b * W:(b + 1) * W] = plain[b * SLOTS:(b + 1) * SLOTS]
        mine = routed[pl.ds(c * SLOTS, SLOTS), :]
        raw_blk = lax.dot_general(mine, p_ref[...], contract, preferred_element_type=F32)
        raw_pool = lax.dot_general(mine, pool[...], contract, preferred_element_type=F32)
        expand = onehot((iota((SLOTS, PER), 0) >> 2) == iota((SLOTS, PER), 1))
        got = mrcv[pl.ds(c * PER, PER), 0, :].astype(BF16)
        got = jnp.dot(expand, got, preferred_element_type=F32)
        lanes, rank = iota((SLOTS, 128), 1), iota((SLOTS, 128), 0) & 3

        def column(f):
            return jnp.sum(jnp.where(lanes == 4 * f + rank, got, 0.0), axis=1, keepdims=True)

        first, second, place, weight = column(0), column(1), column(2), column(3)
        cand = iota((SLOTS, TP), 1)
        block = (cand >> 6).astype(F32)
        allowed = (block == first) | (block == second)
        hit = cand.astype(F32) == first * BLOCK + place
        score_blk = factor * raw_blk
        score_pool = factor * raw_pool
        peak = jnp.maximum(
            jnp.max(jnp.where(allowed, score_blk, -jnp.inf), axis=1, keepdims=True),
            jnp.max(score_pool, axis=1, keepdims=True),
        )
        exp_blk = jnp.where(allowed, jnp.exp(jnp.where(allowed, score_blk - peak, 0.0)), 0.0)
        exp_pool = jnp.exp(score_pool - peak)
        total = jnp.sum(exp_blk, axis=1, keepdims=True) + jnp.sum(exp_pool, axis=1, keepdims=True)
        log_total = peak + jnp.log(total)
        score_pos = jnp.sum(jnp.where(hit, score_blk, 0.0), axis=1, keepdims=True)
        loss_sum = loss_sum + jnp.sum(weight * (log_total - score_pos), axis=0, keepdims=True)
        grad_blk = weight * (exp_blk / total - jnp.where(hit, 1.0, 0.0))
        grad_pool = weight * (exp_pool / total)
        both = jnp.sum(grad_blk * raw_blk, axis=1, keepdims=True) + jnp.sum(grad_pool * raw_pool, axis=1, keepdims=True)
        scale_sum = scale_sum + INV_ROOT * jnp.sum(both, axis=0, keepdims=True)
        low[pl.ds(c * SLOTS, SLOTS), 0:TP] = grad_blk
        low[pl.ds(c * SLOTS, SLOTS), 256:256 + POOL] = grad_pool
        low_blk, low_pool = grad_blk.astype(BF16), grad_pool.astype(BF16)
        for b in range(4):
            cols = slice(b * W, (b + 1) * W)
            part = jnp.dot(low_blk, p_ref[:, cols], preferred_element_type=F32)
            part = part + jnp.dot(low_pool, pool[:, cols], preferred_element_type=F32)
            stack[b * SLOTS:(b + 1) * SLOTS, :] = (factor * part).astype(BF16)
        mixed = jnp.dot(mix, stack[...], preferred_element_type=F32).astype(BF16)
        gsnd[pl.ds(c * PER, PER)] = mixed.reshape(PER, 16, W)
        return loss_sum, scale_sum

    def bundles(ref, c):
        lo = 1 if c == 0 else c * PER
        return ref.at[pl.ds(lo, (c + 1) * PER - lo)]

    def owner_step(c, sums):
        some = bundles(rcv, c)
        copy(some, some, d_send, d_recv.at[c], here).wait_recv()
        some = bundles(mrcv, c)
        copy(some, some, m_send, m_recv.at[c], here).wait_recv()
        sums = work(c, sums)

        def back(o, carry):
            dz, dx = offset(o)
            copy(gsnd.at[o], grcv.at[o], g_send, g_recv.at[o // PER], cluster_peer(-dz, -dx)).start()
            return carry

        lax.fori_loop(1 if c == 0 else c * PER, (c + 1) * PER, back, 0)
        return sums

    sums = (jnp.zeros((1, 1), F32), jnp.zeros((1, 1), F32))
    for c in range(CHUNKS):
        sums = owner_step(c, sums)
    grcv[0] = gsnd[0]

    low[:, TP:256] = jnp.zeros((256, 256 - TP), F32)
    lowt[...] = low[...].T.astype(BF16)

    def pool_term(k, carry):
        cols = pl.ds(pl.multiple_of(k * 512, 512), 512)
        part = jnp.dot(lowt[256:256 + POOL, :], routed[:, cols], preferred_element_type=F32)
        pt[k % 2, k // 2] = factor * part
        return carry

    lax.fori_loop(0, 8, pool_term, 0)
    tile_lane = iota((8, 128), 1)
    sc[0] = jnp.where(tile_lane == 0, sums[0], jnp.where(tile_lane == 1, sums[1], 0.0))

    peer = group_peer(y, 1 - core)
    move = [
        copy(pt.at[1 - core], rc, r_send.at[0], r_recv.at[0], peer),
        copy(sc.at[0], rcs, t_send.at[0], t_recv.at[0], peer),
    ]
    for one in move:
        one.start()

    def passage_term(k, carry):
        cols = pl.ds(pl.multiple_of(k * 512, 512), 512)
        part = jnp.dot(lowt[0:TP, :], routed[:, cols], preferred_element_type=F32)
        pg_ref[:, cols] = (factor * part).astype(BF16)
        return carry

    lax.fori_loop(0, 8, passage_term, 0)
    for one in move:
        one.wait()
    s1[...] = pt[core] + rc[...]
    sc[1] = sc[0] + rcs[...]

    for k in range(1, NY):
        to = (y + k) % NY
        copy(s1.at[to], ry.at[k - 1], r_send.at[1], r_recv.at[1], group_peer(to, core)).start()
        copy(sc.at[1], rys.at[k - 1], t_send.at[1], t_recv.at[1], group_peer(to, core)).start()
    copy(ry, ry, r_send.at[1], r_recv.at[1], here).wait()
    copy(rys, rys, t_send.at[1], t_recv.at[1], here).wait()
    s2[...] = (s1[y] + ry[0] + ry[1] + ry[2]).reshape(NX, 32, 512)
    sc[2] = sc[1] + rys[0] + rys[1] + rys[2]

    for k in range(1, NX):
        to = (x + k) % NX
        copy(s2.at[to], rx.at[k - 1], r_send.at[2], r_recv.at[2], cluster_peer(0, k)).start()
        copy(sc.at[2], rxs.at[k - 1], t_send.at[2], t_recv.at[2], cluster_peer(0, k)).start()
    copy(rx, rx, r_send.at[2], r_recv.at[2], here).wait()
    copy(rxs, rxs, t_send.at[2], t_recv.at[2], here).wait()
    s3 = s2[x] + rx[0] + rx[1] + rx[2]
    scalars = sc[2] + rxs[0] + rxs[1] + rxs[2]
    for r in range(2):
        for cb in range(4):
            zb[:, r * 4 + cb, :] = s3[r * NZ:(r + 1) * NZ, cb * 128:(cb + 1) * 128]
    zb[:, 8:16, :] = jnp.broadcast_to(scalars[None], (NZ, 8, 128))

    def to_z(k, carry):
        copy(zb.at[(z + k) % NZ], rz.at[k - 1], r_send.at[3], r_recv.at[3], cluster_peer(k, 0)).start()
        return carry

    lax.fori_loop(1, NZ, to_z, 0)
    copy(rz, rz, r_send.at[3], r_recv.at[3], here).wait()
    last = zb[z] + jnp.sum(rz[...], axis=0)
    fin[...] = last[0:8]
    gb[grp] = last[0:8]
    loss_ref[0] = jnp.sum(jnp.where(tile_lane[0:1] == 0, last[8:9], 0.0)) * (1.0 / (TQ * OWNERS * 8))
    sgrad_ref[0] = jnp.sum(jnp.where(tile_lane[0:1] == 1, last[8:9], 0.0))

    def to_group(k, carry):
        copy(fin, gb.at[grp], r_send.at[4], r_recv.at[4], ((grp + k) % 8, clu)).start()
        return carry

    lax.fori_loop(1, 8, to_group, 0)

    def take(c):
        some = bundles(grcv, c)
        copy(some, some, g_send, g_recv.at[c], here).wait_recv()
        rows = grcv[pl.ds(c * PER, PER)].reshape(PER * 16, W)
        lanes = iota((TQ, PER * 16), 1) + c * (PER * 16)
        for b in range(4):
            part = jnp.dot(onehot(lanes == place_col + 4 * b), rows, preferred_element_type=F32)
            if c == 0:
                acc[:, b * W:(b + 1) * W] = part
            elif c + 1 < CHUNKS:
                acc[:, b * W:(b + 1) * W] += part
            else:
                home_ref[:, b * W:(b + 1) * W] = (acc[:, b * W:(b + 1) * W] + part).astype(BF16)

    for c in range(CHUNKS):
        take(c)

    some = gb.at[pl.ds(0, 7)]
    copy(some, some, r_send.at[4], r_recv.at[4], here).wait()
    for g in range(8):
        for r in range(2):
            for cb in range(4):
                col = g * 512 + cb * 128
                poolg_ref[r:r + 1, col:col + 128] = gb[g, r * 4 + cb:r * 4 + cb + 1, :]

    some = rcv.at[pl.ds(1, OWNERS - 1)]
    copy(some, some, d_send, d_recv.at[0], here).wait_send()
    copy(some, some, g_send, g_recv.at[0], here).wait_send()
    some = mrcv.at[pl.ds(1, OWNERS - 1)]
    copy(some, some, m_send, m_recv.at[0], here).wait_send()


BASE = 2
V = D // 8
SPARE = 12
RING = 4 * SPARE
LATE = 2 * NZ


def fast_kernel(
    q_ref, cl_ref, bl_ref, pos_ref, p_ref, piece_ref, scale_ref,
    home_ref, pg_ref, poolg_ref, loss_ref, sgrad_ref, flag_ref,
    snd, rcv, msnd, mrcv, gsnd, grcv, stack, routed, low, lowt, acc, gp, pool,
    og, tg, px, pv, pts, ptr, rsn, rv, cc, rr, ll, late,
    pt, rc, s1, ry, s2, rx, zb, rz, fin, gb, sc, rcs, rys, rxs,
    d_send, d_recv, m_send, m_recv, g_send, g_recv, p_send, p_recv, r_send, r_recv, t_send, t_recv,
    f_send, fr_recv, fl_recv, b_send, br_recv, bl_recv, x_send, x_recv,
):
    grp = lax.axis_index("group")
    clu = lax.axis_index("cluster")
    y, core = grp // 2, grp % 2
    z, x = clu // NX, clu % NX

    def cluster_peer(dz, dx):
        return (grp, ((z + dz + NZ) % NZ) * NX + (x + dx + NX) % NX)

    def group_peer(py, pc):
        return (py * 2 + pc, clu)

    def offset(o):
        return ((o // 4) % 4) * 4 + o // 16, o % 4

    def copy(src, dst, send, recv, peer):
        return pltpu.make_async_remote_copy(
            src_ref=src, dst_ref=dst, send_sem=send, recv_sem=recv, device_id=peer, device_id_type=MESH
        )

    here = (grp, clu)
    barrier = pltpu.get_barrier_semaphore()

    def greet(o, carry):
        dz, dx = offset(o)
        pl.semaphore_signal(barrier, inc=1, device_id=cluster_peer(dz, dx), device_id_type=MESH)
        return carry

    lax.fori_loop(1, OWNERS, greet, 0)

    def greet_group(k, carry):
        pl.semaphore_signal(barrier, inc=1, device_id=((grp + k) % 8, clu), device_id_type=MESH)
        return carry

    lax.fori_loop(1, 8, greet_group, 0)

    factor = scale_ref[0] * INV_ROOT

    a_iota, b_iota = iota((TQ, TQ), 0), iota((TQ, TQ), 1)
    eye = a_iota == b_iota

    def to_col(row):
        return jnp.sum(jnp.where(eye, row.astype(F32), 0.0), axis=1, keepdims=True)

    cl_row = cl_ref[...]
    cl_col = to_col(cl_row).astype(jnp.int32)
    same = cl_col == cl_row
    rank_row = jnp.sum(jnp.where(same & (a_iota < b_iota), 1.0, 0.0), axis=0, keepdims=True).astype(jnp.int32)
    rank_col = jnp.sum(jnp.where(same & (b_iota < a_iota), 1.0, 0.0), axis=1, keepdims=True).astype(jnp.int32)
    extra_row, extra_col = rank_row >= BASE, rank_col >= BASE
    spare_row = jnp.sum(jnp.where(extra_col & (a_iota < b_iota), 1.0, 0.0), axis=0, keepdims=True).astype(jnp.int32)
    spare_col = jnp.sum(jnp.where(extra_row & (b_iota < a_iota), 1.0, 0.0), axis=1, keepdims=True).astype(jnp.int32)
    fits_row, fits_col = extra_row & (spare_row < SPARE), extra_col & (spare_col < SPARE)
    spare_row = jnp.where(fits_row, spare_row, -4096)
    spare_col = jnp.where(fits_col, spare_col, -4096)
    left_over = jnp.sum(jnp.where(extra_col & jnp.logical_not(fits_col), 1.0, 0.0), axis=0, keepdims=True)

    def offset_of(cl):
        dz = ((cl >> 2) - z) & 15
        return (dz & 3) * 16 + (dz >> 2) * 4 + ((cl - x) & 3)

    off_row, off_col = offset_of(cl_row), offset_of(cl_col)
    place_row = jnp.where(extra_row, -4096, off_row * 16 + rank_row)
    place_col = jnp.where(extra_col, -4096, off_col * 16 + rank_col)

    lane = iota((TQ, 128), 1)
    field = lane >> 2
    block0, block1, position = to_col(bl_ref[0:1, :]), to_col(bl_ref[1:2, :]), to_col(pos_ref[...])
    value = jnp.where(field == 0, block0, jnp.where(field == 1, block1, jnp.where(field == 2, position, 1.0)))
    value = jnp.where((rank_col == (lane & 3)) & (field < 4) & jnp.logical_not(extra_col), value, 0.0).astype(BF16)
    meta = jnp.dot(onehot(iota((OWNERS, TQ), 0) == off_row), value, preferred_element_type=F32)
    msnd[:, 0, :] = meta

    total = jnp.zeros((RING, W), F32)
    for b in range(4):
        pick = onehot(iota((RING, TQ), 0) == spare_row + SPARE * b)
        total = total + jnp.dot(pick, q_ref[:, b * W:(b + 1) * W], preferred_element_type=F32)
    og[z] = total.astype(BF16)
    kind = iota((8, TQ), 0)
    facts = jnp.where(
        kind == 0, cl_row.astype(F32),
        jnp.where(
            kind == 1, bl_ref[0:1, :].astype(F32),
            jnp.where(kind == 2, bl_ref[1:2, :].astype(F32), jnp.where(kind == 3, pos_ref[...].astype(F32), 1.0)),
        ),
    )
    facts = jnp.where(kind < 5, facts, 0.0).astype(BF16)
    spot = lane % SPARE
    tg[z] = jnp.dot(facts, onehot((spot == spare_col) & (lane < RING)), preferred_element_type=F32)

    def build(c):
        row = iota((PER * 16, TQ), 0) + c * (PER * 16)
        total = jnp.zeros((PER * 16, V), F32)
        for b in range(8):
            pick = onehot(row == place_row + BASE * b)
            total = total + jnp.dot(pick, q_ref[:, b * V:(b + 1) * V], preferred_element_type=F32)
        snd[pl.ds(c * PER, PER)] = total.astype(BF16).reshape(PER, 16, V)

    def send_chunk(c):
        def step(o, carry):
            dz, dx = offset(o)
            peer = cluster_peer(dz, dx)
            copy(msnd.at[o], mrcv.at[o], m_send, m_recv.at[o // PER], peer).start()
            copy(snd.at[o], rcv.at[o], d_send, d_recv.at[o // PER], peer).start()
            return carry

        lax.fori_loop(1 if c == 0 else c * PER, (c + 1) * PER, step, 0)

    def right(k):
        one = og.at[(z - k + 1 + NZ) % NZ]
        return copy(one, one, f_send.at[0], fr_recv.at[k - 1], cluster_peer(1, 0))

    def left(k):
        one = og.at[(z + k - 1) % NZ]
        return copy(one, one, f_send.at[1], fl_recv.at[k - 1], cluster_peer(-1, 0))

    def ring(k):
        if k > 1:
            one = og.at[(z - k + 1 + NZ) % NZ]
            copy(one, one, f_send.at[0], fr_recv.at[k - 2], here).wait_recv()
            one = og.at[(z + k - 1) % NZ]
            copy(one, one, f_send.at[1], fl_recv.at[k - 2], here).wait_recv()
        right(k).start()
        if k < 8:
            left(k).start()

    gp[y, x, z] = piece_ref[y]
    pl.semaphore_wait(barrier, OWNERS - 1 + 7)
    ring(1)

    def early(k, carry):
        copy(tg.at[z], tg.at[z], t_send.at[3], t_recv.at[3], cluster_peer(k, 0)).start()
        copy(gp.at[y, x, z], gp.at[y, x, z], p_send.at[0], p_recv.at[0], cluster_peer(k, 0)).start()
        return carry

    lax.fori_loop(1, NZ, early, 0)
    build(0)
    send_chunk(0)
    build(1)
    ring(2)
    some = gp.at[y, x, pl.ds(0, NZ - 1)]
    copy(some, some, p_send.at[0], p_recv.at[0], here).wait()
    for k in range(1, NX):
        copy(gp.at[y, x], gp.at[y, x], p_send.at[1], p_recv.at[1], cluster_peer(0, k)).start()
    ring(3)
    send_chunk(1)
    build(2)
    ring(4)
    some = gp.at[y, pl.ds(0, NX - 1)]
    copy(some, some, p_send.at[1], p_recv.at[1], here).wait()
    for k in range(1, NY):
        copy(gp.at[y], gp.at[y], p_send.at[2], p_recv.at[2], group_peer((y + k) % NY, core)).start()
    ring(5)
    send_chunk(2)
    build(3)
    ring(6)
    rcv[0] = snd[0]
    mrcv[0] = msnd[0]
    some = gp.at[pl.ds(0, NY - 1)]
    copy(some, some, p_send.at[2], p_recv.at[2], here).wait()

    def spread(yy, carry):
        flat = gp[yy].reshape(OWNERS * 16, 128)
        i, j = iota((POOL, OWNERS * 16), 0), iota((POOL, OWNERS * 16), 1)
        base = (i >> 5) * (NZ * 16) + (i & 15) * 16 + ((i >> 4) & 1) * 8
        for cb in range(8):
            part = jnp.dot(onehot(j == base + cb), flat, preferred_element_type=F32).astype(BF16)
            pool[:, pl.ds(pl.multiple_of(yy * W + cb * 128, 128), 128)] = part
        return carry

    some = tg.at[pl.ds(0, NZ - 1)]
    copy(some, some, t_send.at[3], t_recv.at[3], here).wait()

    ring(7)
    send_chunk(3)
    lax.fori_loop(0, NY, spread, 0)

    def gather_facts(k, carry):
        shift = onehot((iota((128, NZ * RING), 1) == iota((128, NZ * RING), 0) + k * RING) & (iota((128, NZ * RING), 0) < RING))
        return carry + jnp.dot(tg[k].astype(BF16), shift, preferred_element_type=F32)

    span = NZ * RING
    known = lax.fori_loop(0, NZ, gather_facts, jnp.zeros((8, span), F32))
    dest = known[0:1].astype(jnp.int32)
    local = (known[4:5] > 0.5) & ((dest >> 2) == z)
    across = iota((1, span), 1)
    block_of = (across % RING) // SPARE
    to_x = dest & 3
    mark = (iota((8, span), 0) == to_x) & local & (block_of == 0)
    before = onehot(iota((span, span), 0) < across - block_of * SPARE)
    ranks = jnp.dot(onehot(mark), before, preferred_element_type=F32)
    order = jnp.sum(jnp.where(iota((8, span), 0) == to_x, ranks, 0.0), axis=0, keepdims=True).astype(jnp.int32)
    key = jnp.where(local, to_x * (4 * LATE) + block_of * LATE + order, -1)
    first_key = jnp.where(local & (block_of == 0), to_x * LATE + order, -1)
    key_col = jnp.broadcast_to(key.astype(F32), (8, span)).T[:, 0:1].astype(jnp.int32)
    pts[...] = lax.dot_general(
        known.astype(BF16), onehot(iota((NX * LATE, span), 0) == first_key), (((1,), (1,)), ((), ())),
        preferred_element_type=F32,
    )
    ring(8)
    one = og.at[(z + 8) % NZ]
    copy(one, one, f_send.at[0], fr_recv.at[7], here).wait_recv()
    for to in range(NX):
        pick = onehot(iota((4 * LATE, span), 0) + to * (4 * LATE) == key)
        px[to] = jnp.dot(pick, og[...].reshape(span, W), preferred_element_type=F32).astype(BF16)
    for k in range(1, NX):
        copy(px.at[(x + k) % NX], pv.at[x], x_send.at[0], x_recv.at[0], cluster_peer(0, k)).start()
        copy(pts, ptr.at[x], x_send.at[1], x_recv.at[1], cluster_peer(0, k)).start()
    pv[x] = px[x]
    ptr[x] = pts[...]

    i, j = iota((256, 256), 0), iota((256, 256), 1)
    unmix = onehot(((i >> 1) & 15) * 16 + (i >> 5) * 2 + (i & 1) == j)
    mix = onehot(((j >> 1) & 15) * 16 + (j >> 5) * 2 + (j & 1) == i)
    contract = (((1,), (1,)), ((), ()))

    def work(lo, count, columns, sums):
        loss_sum, scale_sum = sums
        first, second, place, weight = columns
        mine = routed[lo:lo + count, :]
        raw_blk = lax.dot_general(mine, p_ref[...], contract, preferred_element_type=F32)
        raw_pool = lax.dot_general(mine, pool[...], contract, preferred_element_type=F32)
        cand = iota((count, TP), 1)
        block = (cand >> 6).astype(F32)
        allowed = (block == first) | (block == second)
        hit = cand.astype(F32) == first * BLOCK + place
        score_blk = factor * raw_blk
        score_pool = factor * raw_pool
        peak = jnp.maximum(
            jnp.max(jnp.where(allowed, score_blk, -jnp.inf), axis=1, keepdims=True),
            jnp.max(score_pool, axis=1, keepdims=True),
        )
        exp_blk = jnp.where(allowed, jnp.exp(jnp.where(allowed, score_blk - peak, 0.0)), 0.0)
        exp_pool = jnp.exp(score_pool - peak)
        total = jnp.sum(exp_blk, axis=1, keepdims=True) + jnp.sum(exp_pool, axis=1, keepdims=True)
        log_total = peak + jnp.log(total)
        score_pos = jnp.sum(jnp.where(hit, score_blk, 0.0), axis=1, keepdims=True)
        loss_sum = loss_sum + jnp.sum(weight * (log_total - score_pos), axis=0, keepdims=True)
        grad_blk = weight * (exp_blk / total - jnp.where(hit, 1.0, 0.0))
        grad_pool = weight * (exp_pool / total)
        both = jnp.sum(grad_blk * raw_blk, axis=1, keepdims=True) + jnp.sum(grad_pool * raw_pool, axis=1, keepdims=True)
        scale_sum = scale_sum + INV_ROOT * jnp.sum(both, axis=0, keepdims=True)
        low[lo:lo + count, 0:TP] = grad_blk
        low[lo:lo + count, 256:256 + POOL] = grad_pool
        low_blk, low_pool = grad_blk.astype(BF16), grad_pool.astype(BF16)

        def grads(cols):
            part = jnp.dot(low_blk, p_ref[:, cols], preferred_element_type=F32)
            part = part + jnp.dot(low_pool, pool[:, cols], preferred_element_type=F32)
            return (factor * part).astype(BF16)

        return (loss_sum, scale_sum), grads

    def bundles(ref, c):
        lo = 1 if c == 0 else c * PER
        return ref.at[pl.ds(lo, (c + 1) * PER - lo)]

    HALF = 2 * PER * BASE

    def half(h, sums):
        for c in (2 * h, 2 * h + 1):
            some = bundles(rcv, c)
            copy(some, some, d_send, d_recv.at[c], here).wait_recv()
            some = bundles(mrcv, c)
            copy(some, some, m_send, m_recv.at[c], here).wait_recv()
            rows = rcv[pl.ds(c * PER, PER)].reshape(PER * 16, V)
            plain = jnp.dot(unmix, rows, preferred_element_type=F32).astype(BF16)
            for b in range(8):
                routed[c * 32:(c + 1) * 32, b * V:(b + 1) * V] = plain[b * 32:(b + 1) * 32]
        expand = onehot((iota((HALF, 2 * PER), 0) >> 1) == iota((HALF, 2 * PER), 1))
        got = mrcv[pl.ds(2 * h * PER, 2 * PER), 0, :].astype(BF16)
        got = jnp.dot(expand, got, preferred_element_type=F32)
        lanes, rank = iota((HALF, 128), 1), iota((HALF, 128), 0) & 1

        def column(f):
            return jnp.sum(jnp.where(lanes == 4 * f + rank, got, 0.0), axis=1, keepdims=True)

        sums, grads = work(h * HALF, HALF, [column(f) for f in range(4)], sums)
        for b in range(8):
            part = grads(slice(b * V, (b + 1) * V))
            stack[0, b * 32:(b + 1) * 32, :] = part[0:32]
            stack[1, b * 32:(b + 1) * 32, :] = part[32:64]
        for c in (0, 1):
            mixed = jnp.dot(mix, stack[c], preferred_element_type=F32).astype(BF16)
            gsnd[pl.ds((2 * h + c) * PER, PER)] = mixed.reshape(PER, 16, V)
        return sums

    def send_back(c):
        def back(o, carry):
            dz, dx = offset(o)
            copy(gsnd.at[o], grcv.at[o], g_send, g_recv.at[o // PER], cluster_peer(-dz, -dx)).start()
            return carry

        lax.fori_loop(1 if c == 0 else c * PER, (c + 1) * PER, back, 0)

    sums = (jnp.zeros((1, 1), F32), jnp.zeros((1, 1), F32))
    sums = half(0, sums)
    send_back(0)
    send_back(1)
    grcv[0] = gsnd[0]

    some = pv.at[pl.ds(0, NX - 1)]
    copy(some, some, x_send.at[0], x_recv.at[0], here).wait()
    some = ptr.at[pl.ds(0, NX - 1)]
    copy(some, some, x_send.at[1], x_recv.at[1], here).wait()
    choose = onehot(iota((LATE, 128), 1) == iota((LATE, 128), 0) + x * LATE)
    for via in range(NX):
        for b in range(4):
            routed[128 + via * LATE:128 + (via + 1) * LATE, b * W:(b + 1) * W] = pv[via, b * LATE:(b + 1) * LATE, :]
        late[via * LATE:(via + 1) * LATE, 0:8] = lax.dot_general(
            choose, ptr[via].astype(BF16), contract, preferred_element_type=F32
        )
    sums, grads = work(128, 128, [late[:, f:f + 1] for f in range(1, 5)], sums)
    for b in range(4):
        part = grads(slice(b * W, (b + 1) * W))
        for via in range(NX):
            rsn[via, b * LATE:(b + 1) * LATE, :] = part[via * LATE:(via + 1) * LATE]
    for k in range(1, NX):
        copy(rsn.at[(x + k) % NX], rv.at[x], x_send.at[2], x_recv.at[2], cluster_peer(0, k)).start()
    rv[x] = rsn[x]
    sums = half(1, sums)

    some = rv.at[pl.ds(0, NX - 1)]
    copy(some, some, x_send.at[2], x_recv.at[2], here).wait()
    cols_iota = iota((RING, NX * 4 * LATE), 1)
    for k in range(NZ):
        pick = onehot(cols_iota == key_col[k * RING:(k + 1) * RING])
        cc[k] = jnp.dot(pick, rv[...].reshape(NX * 4 * LATE, W), preferred_element_type=F32).astype(BF16)

    def ring_back(k):
        to = (z + 9 - k) % NZ
        if k > 1:
            copy(rr.at[k - 2], rr.at[k - 2], b_send.at[0], br_recv.at[k - 2], here).wait_recv()
            cc[to] = cc[to] + rr[k - 2]
        copy(cc.at[to], rr.at[k - 1], b_send.at[0], br_recv.at[k - 1], cluster_peer(1, 0)).start()
        if k < 8:
            to = (z - 8 + k + NZ) % NZ
            if k > 1:
                copy(ll.at[k - 2], ll.at[k - 2], b_send.at[1], bl_recv.at[k - 2], here).wait_recv()
                cc[to] = cc[to] + ll[k - 2]
            copy(cc.at[to], ll.at[k - 1], b_send.at[1], bl_recv.at[k - 1], cluster_peer(-1, 0)).start()

    ring_back(1)
    send_back(2)

    low[:, TP:256] = jnp.zeros((256, 256 - TP), F32)
    lowt[...] = low[...].T.astype(BF16)

    def pool_term(k, carry):
        cols = pl.ds(pl.multiple_of(k * 512, 512), 512)
        part = jnp.dot(lowt[256:256 + POOL, :], routed[:, cols], preferred_element_type=F32)
        pt[k % 2, k // 2] = factor * part
        return carry

    lax.fori_loop(0, 8, pool_term, 0)
    tile_lane = iota((8, 128), 1)
    sc[0] = jnp.where(
        tile_lane == 0, sums[0], jnp.where(tile_lane == 1, sums[1], jnp.where(tile_lane == 2, left_over, 0.0))
    )

    peer = group_peer(y, 1 - core)
    move = [
        copy(pt.at[1 - core], rc, r_send.at[0], r_recv.at[0], peer),
        copy(sc.at[0], rcs, t_send.at[0], t_recv.at[0], peer),
    ]
    for one in move:
        one.start()
    ring_back(2)
    send_back(3)

    def passage_term(k, carry):
        cols = pl.ds(pl.multiple_of(k * 512, 512), 512)
        part = jnp.dot(lowt[0:TP, :], routed[:, cols], preferred_element_type=F32)
        pg_ref[:, cols] = (factor * part).astype(BF16)
        return carry

    lax.fori_loop(0, 8, passage_term, 0)
    for one in move:
        one.wait()
    s1[...] = pt[core] + rc[...]
    sc[1] = sc[0] + rcs[...]

    for k in range(1, NY):
        to = (y + k) % NY
        copy(s1.at[to], ry.at[k - 1], r_send.at[1], r_recv.at[1], group_peer(to, core)).start()
        copy(sc.at[1], rys.at[k - 1], t_send.at[1], t_recv.at[1], group_peer(to, core)).start()
    ring_back(3)
    copy(ry, ry, r_send.at[1], r_recv.at[1], here).wait()
    copy(rys, rys, t_send.at[1], t_recv.at[1], here).wait()
    s2[...] = (s1[y] + ry[0] + ry[1] + ry[2]).reshape(NX, 32, 512)
    sc[2] = sc[1] + rys[0] + rys[1] + rys[2]

    for k in range(1, NX):
        to = (x + k) % NX
        copy(s2.at[to], rx.at[k - 1], r_send.at[2], r_recv.at[2], cluster_peer(0, k)).start()
        copy(sc.at[2], rxs.at[k - 1], t_send.at[2], t_recv.at[2], cluster_peer(0, k)).start()
    ring_back(4)
    copy(rx, rx, r_send.at[2], r_recv.at[2], here).wait()
    copy(rxs, rxs, t_send.at[2], t_recv.at[2], here).wait()
    s3 = s2[x] + rx[0] + rx[1] + rx[2]
    scalars = sc[2] + rxs[0] + rxs[1] + rxs[2]
    for r in range(2):
        for cb in range(4):
            zb[:, r * 4 + cb, :] = s3[r * NZ:(r + 1) * NZ, cb * 128:(cb + 1) * 128]
    zb[:, 8:16, :] = jnp.broadcast_to(scalars[None], (NZ, 8, 128))

    def to_z(k, carry):
        copy(zb.at[(z + k) % NZ], rz.at[k - 1], r_send.at[3], r_recv.at[3], cluster_peer(k, 0)).start()
        return carry

    lax.fori_loop(1, NZ, to_z, 0)
    ring_back(5)
    ring_back(6)
    copy(rz, rz, r_send.at[3], r_recv.at[3], here).wait()
    last = zb[z] + jnp.sum(rz[...], axis=0)
    fin[...] = last[0:8]
    gb[grp] = last[0:8]
    loss_ref[0] = jnp.sum(jnp.where(tile_lane[0:1] == 0, last[8:9], 0.0)) * (1.0 / (TQ * OWNERS * 8))
    sgrad_ref[0] = jnp.sum(jnp.where(tile_lane[0:1] == 1, last[8:9], 0.0))
    flag_ref[0] = jnp.sum(jnp.where(tile_lane[0:1] == 2, last[8:9], 0.0))

    def to_group(k, carry):
        copy(fin, gb.at[grp], r_send.at[4], r_recv.at[4], ((grp + k) % 8, clu)).start()
        return carry

    lax.fori_loop(1, 8, to_group, 0)
    ring_back(7)

    def take(c):
        some = bundles(grcv, c)
        copy(some, some, g_send, g_recv.at[c], here).wait_recv()
        rows = grcv[pl.ds(c * PER, PER)].reshape(PER * 16, V)
        lanes = iota((TQ, PER * 16), 1) + c * (PER * 16)
        for b in range(8):
            part = jnp.dot(onehot(lanes == place_col + BASE * b), rows, preferred_element_type=F32)
            if c == 0:
                acc[:, b * V:(b + 1) * V] = part
            else:
                acc[:, b * V:(b + 1) * V] += part

    take(0)
    ring_back(8)
    for c in range(1, CHUNKS):
        take(c)
    copy(rr.at[7], rr.at[7], b_send.at[0], br_recv.at[7], here).wait_recv()
    copy(ll.at[6], ll.at[6], b_send.at[1], bl_recv.at[6], here).wait_recv()
    spare_rows = cc[z] + rr[7] + ll[6]
    for b in range(4):
        pick = onehot(iota((TQ, RING), 1) == spare_col + SPARE * b)
        part = jnp.dot(pick, spare_rows, preferred_element_type=F32)
        home_ref[:, b * W:(b + 1) * W] = (acc[:, b * W:(b + 1) * W] + part).astype(BF16)

    some = gb.at[pl.ds(0, 7)]
    copy(some, some, r_send.at[4], r_recv.at[4], here).wait()
    for g in range(8):
        for r in range(2):
            for cb in range(4):
                col = g * 512 + cb * 128
                poolg_ref[r:r + 1, col:col + 128] = gb[g, r * 4 + cb:r * 4 + cb + 1, :]

    some = rcv.at[pl.ds(1, OWNERS - 1)]
    copy(some, some, d_send, d_recv.at[0], here).wait_send()
    copy(some, some, g_send, g_recv.at[0], here).wait_send()
    some = mrcv.at[pl.ds(1, OWNERS - 1)]
    copy(some, some, m_send, m_recv.at[0], here).wait_send()
    for side, count in ((0, 8), (1, 7)):
        some = og.at[pl.ds(0, count)]
        copy(some, some, f_send.at[side], fr_recv.at[0], here).wait_send()
        some = cc.at[pl.ds(0, count)]
        copy(some, some, b_send.at[side], br_recv.at[0], here).wait_send()


def reduce_scratch():
    return [
        pltpu.VMEM((2, NY, POOL, 512), F32),
        pltpu.VMEM((NY, POOL, 512), F32),
        pltpu.VMEM((NY, POOL, 512), F32),
        pltpu.VMEM((NY - 1, POOL, 512), F32),
        pltpu.VMEM((NX, 32, 512), F32),
        pltpu.VMEM((NX - 1, 32, 512), F32),
        pltpu.VMEM((NZ, 16, 128), F32),
        pltpu.VMEM((NZ - 1, 16, 128), F32),
        pltpu.VMEM((8, 128), F32),
        pltpu.VMEM((8, 8, 128), F32),
        pltpu.VMEM((3, 8, 128), F32),
        pltpu.VMEM((8, 128), F32),
        pltpu.VMEM((NY - 1, 8, 128), F32),
        pltpu.VMEM((NX - 1, 8, 128), F32),
    ]


def fast_call(*args):
    vm = pl.BlockSpec(memory_space=pltpu.VMEM)
    sm = pl.BlockSpec(memory_space=pltpu.SMEM)
    bundle = pltpu.VMEM((OWNERS, 16, V), BF16)
    note = pltpu.VMEM((OWNERS, 1, 128), F32)
    column = pltpu.VMEM((NX, 4 * LATE, W), BF16)
    dma = pltpu.SemaphoreType.DMA
    scalar = jax.ShapeDtypeStruct((1,), F32)
    return pl.pallas_call(
        fast_kernel,
        out_shape=(
            jax.ShapeDtypeStruct((TQ, D), BF16),
            jax.ShapeDtypeStruct((TP, D), BF16),
            jax.ShapeDtypeStruct((2, D), F32),
            scalar, scalar, scalar,
        ),
        in_specs=[vm] * 6 + [sm],
        out_specs=(vm, vm, vm, sm, sm, sm),
        scratch_shapes=[
            bundle, bundle, note, note, bundle, bundle,
            pltpu.VMEM((2, 256, V), BF16),
            pltpu.VMEM((256, D), BF16),
            pltpu.VMEM((256, 384), F32),
            pltpu.VMEM((384, 256), BF16),
            pltpu.VMEM((TQ, D), F32),
            pltpu.VMEM((NY, NX, NZ, 16, 128), BF16),
            pltpu.VMEM((POOL, D), BF16),
            pltpu.VMEM((NZ, RING, W), BF16),
            pltpu.VMEM((NZ, 8, 128), F32),
            column, column,
            pltpu.VMEM((8, 128), F32),
            pltpu.VMEM((NX, 8, 128), F32),
            column, column,
            pltpu.VMEM((NZ, RING, W), BF16),
            pltpu.VMEM((8, RING, W), BF16),
            pltpu.VMEM((7, RING, W), BF16),
            pltpu.VMEM((128, 128), F32),
            *reduce_scratch(),
            dma, dma((CHUNKS,)), dma, dma((CHUNKS,)), dma, dma((CHUNKS,)),
            dma((3,)), dma((3,)), dma((5,)), dma((5,)), dma((4,)), dma((4,)),
            dma((2,)), dma((8,)), dma((7,)), dma((2,)), dma((8,)), dma((7,)), dma((3,)), dma((3,)),
        ],
        compiler_params=pltpu.CompilerParams(
            collective_id=1, has_side_effects=True, vmem_limit_bytes=48 * 1024 * 1024
        ),
        cost_estimate=pl.CostEstimate(flops=4 * 10**9, bytes_accessed=6 * 10**6, transcendentals=82000),
    )(*args)


def full_call(*args):
    vm = pl.BlockSpec(memory_space=pltpu.VMEM)
    sm = pl.BlockSpec(memory_space=pltpu.SMEM)
    bundle = pltpu.VMEM((OWNERS, 16, W), BF16)
    note = pltpu.VMEM((OWNERS, 1, 128), F32)
    dma = pltpu.SemaphoreType.DMA
    return pl.pallas_call(
        full_kernel,
        out_shape=(
            jax.ShapeDtypeStruct((TQ, D), BF16),
            jax.ShapeDtypeStruct((TP, D), BF16),
            jax.ShapeDtypeStruct((2, D), F32),
            jax.ShapeDtypeStruct((1,), F32),
            jax.ShapeDtypeStruct((1,), F32),
        ),
        in_specs=[vm] * 6 + [sm],
        out_specs=(vm, vm, vm, sm, sm),
        scratch_shapes=[
            bundle, bundle, note, note, bundle, bundle,
            pltpu.VMEM((256, W), BF16),
            pltpu.VMEM((256, D), BF16),
            pltpu.VMEM((256, 384), F32),
            pltpu.VMEM((384, 256), BF16),
            pltpu.VMEM((TQ, D), F32),
            pltpu.VMEM((NY, NX, NZ, 16, 128), BF16),
            pltpu.VMEM((POOL, D), BF16),
            *reduce_scratch(),
            dma, dma((CHUNKS,)), dma, dma((CHUNKS,)), dma, dma((CHUNKS,)),
            dma((3,)), dma((3,)), dma((5,)), dma((5,)), dma((3,)), dma((3,)),
        ],
        compiler_params=pltpu.CompilerParams(
            collective_id=0, has_side_effects=True, vmem_limit_bytes=48 * 1024 * 1024
        ),
        cost_estimate=pl.CostEstimate(flops=4 * 10**9, bytes_accessed=6 * 10**6, transcendentals=82000),
    )(*args)


def per_device(queries, cluster_id, block_list, positive, passages, pool_rows, logit_scale):
    piece = pool_rows.reshape(2, 4, 8, 128).transpose(1, 0, 2, 3).reshape(4, 16, 128)
    args = (
        queries,
        cluster_id.reshape(1, TQ),
        block_list.T,
        positive.reshape(1, TQ),
        passages,
        piece,
        logit_scale,
    )
    *quick, left_over = fast_call(*args)
    return lax.cond(left_over[0] > 0.5, lambda: tuple(full_call(*args)), lambda: tuple(quick))


def solution(mesh):
    placed = (
        P(("group", "cluster"), None),
        P(("group", "cluster"), None),
        P(("group", "cluster"), None),
        P(("group", "cluster")),
        P(("group", "cluster"), None),
        P("cluster", None),
        P(),
    )
    return jax.shard_map(
        per_device,
        mesh=mesh,
        in_specs=placed,
        out_specs=(
            P(("group", "cluster"), None),
            P(("group", "cluster"), None),
            P("cluster", None),
            P(),
            P(),
        ),
        check_vma=False,
    )
```

```python
import math

import jax
import jax.numpy as jnp
from jax import lax
from jax.experimental import pallas as pl
from jax.experimental.pallas import tpu as pltpu
from jax.sharding import PartitionSpec as P

D = 4096
TQ = 112
BLOCK = 64
TP = 192
POOL = 128
NX = 4
NZ = 16
NY = 4
OWNERS = NX * NZ
CAP = 4
CHUNKS = 4
PER = OWNERS // CHUNKS
SLOTS = PER * CAP
W = D // 4
INV_ROOT = 1.0 / math.sqrt(D)
MESH = pl.DeviceIdType.MESH
F32 = jnp.float32
BF16 = jnp.bfloat16


def iota(shape, axis):
    return lax.broadcasted_iota(jnp.int32, shape, axis)


def onehot(mask):
    return jnp.where(mask, 1.0, 0.0).astype(BF16)


def full_kernel(
    q_ref, cl_ref, bl_ref, pos_ref, p_ref, piece_ref, scale_ref,
    home_ref, pg_ref, poolg_ref, loss_ref, sgrad_ref,
    snd, rcv, msnd, mrcv, gsnd, grcv, stack, routed, low, lowt, acc, gp, pool,
    pt, rc, s1, ry, s2, rx, zb, rz, fin, gb, sc, rcs, rys, rxs,
    d_send, d_recv, m_send, m_recv, g_send, g_recv, p_send, p_recv, r_send, r_recv, t_send, t_recv,
):
    grp = lax.axis_index("group")
    clu = lax.axis_index("cluster")
    y, core = grp // 2, grp % 2
    z, x = clu // NX, clu % NX

    def cluster_peer(dz, dx):
        return (grp, ((z + dz + NZ) % NZ) * NX + (x + dx + NX) % NX)

    def group_peer(py, pc):
        return (py * 2 + pc, clu)

    def offset(o):
        return ((o // 4) % 4) * 4 + o // 16, o % 4

    def copy(src, dst, send, recv, peer):
        return pltpu.make_async_remote_copy(
            src_ref=src, dst_ref=dst, send_sem=send, recv_sem=recv, device_id=peer, device_id_type=MESH
        )

    here = (grp, clu)
    barrier = pltpu.get_barrier_semaphore()

    def greet(o, carry):
        dz, dx = offset(o)
        pl.semaphore_signal(barrier, inc=1, device_id=cluster_peer(dz, dx), device_id_type=MESH)
        return carry

    lax.fori_loop(1, OWNERS, greet, 0)

    def greet_group(k, carry):
        pl.semaphore_signal(barrier, inc=1, device_id=((grp + k) % 8, clu), device_id_type=MESH)
        return carry

    lax.fori_loop(1, 8, greet_group, 0)

    factor = scale_ref[0] * INV_ROOT

    a_iota, b_iota = iota((TQ, TQ), 0), iota((TQ, TQ), 1)
    eye = a_iota == b_iota

    def to_col(row):
        return jnp.sum(jnp.where(eye, row.astype(F32), 0.0), axis=1, keepdims=True)

    cl_row = cl_ref[...]
    cl_col = to_col(cl_row).astype(jnp.int32)
    same = cl_col == cl_row
    rank_row = jnp.sum(jnp.where(same & (a_iota < b_iota), 1.0, 0.0), axis=0, keepdims=True).astype(jnp.int32)
    rank_col = jnp.sum(jnp.where(same & (b_iota < a_iota), 1.0, 0.0), axis=1, keepdims=True).astype(jnp.int32)

    def offset_of(cl):
        dz = ((cl >> 2) - z) & 15
        return (dz & 3) * 16 + (dz >> 2) * 4 + ((cl - x) & 3)

    off_row, off_col = offset_of(cl_row), offset_of(cl_col)
    place_row = off_row * 16 + rank_row
    place_col = off_col * 16 + rank_col

    lane = iota((TQ, 128), 1)
    field = lane >> 2
    block0, block1, position = to_col(bl_ref[0:1, :]), to_col(bl_ref[1:2, :]), to_col(pos_ref[...])
    value = jnp.where(field == 0, block0, jnp.where(field == 1, block1, jnp.where(field == 2, position, 1.0)))
    value = jnp.where((rank_col == (lane & 3)) & (field < 4), value, 0.0).astype(BF16)
    meta = jnp.dot(onehot(iota((OWNERS, TQ), 0) == off_row), value, preferred_element_type=F32)
    msnd[:, 0, :] = meta

    def build(c, carry):
        row = iota((PER * 16, TQ), 0) + c * (PER * 16)
        total = jnp.zeros((PER * 16, W), F32)
        for b in range(4):
            pick = onehot(row == place_row + 4 * b)
            total = total + jnp.dot(pick, q_ref[:, b * W:(b + 1) * W], preferred_element_type=F32)
        snd[pl.ds(c * PER, PER)] = total.astype(BF16).reshape(PER, 16, W)
        return carry

    def send_chunk(c):
        def step(o, carry):
            dz, dx = offset(o)
            peer = cluster_peer(dz, dx)
            copy(msnd.at[o], mrcv.at[o], m_send, m_recv.at[o // PER], peer).start()
            copy(snd.at[o], rcv.at[o], d_send, d_recv.at[o // PER], peer).start()
            return carry

        lax.fori_loop(1 if c == 0 else c * PER, (c + 1) * PER, step, 0)

    build(0, 0)
    gp[y, x, z] = piece_ref[y]
    pl.semaphore_wait(barrier, OWNERS - 1 + 7)

    def pool_z(k, carry):
        copy(gp.at[y, x, z], gp.at[y, x, z], p_send.at[0], p_recv.at[0], cluster_peer(k, 0)).start()
        return carry

    lax.fori_loop(1, NZ, pool_z, 0)
    for c in range(CHUNKS):
        send_chunk(c)
        if c + 1 < CHUNKS:
            build(c + 1, 0)
    rcv[0] = snd[0]
    mrcv[0] = msnd[0]

    some = gp.at[y, x, pl.ds(0, NZ - 1)]
    copy(some, some, p_send.at[0], p_recv.at[0], here).wait()
    for k in range(1, NX):
        copy(gp.at[y, x], gp.at[y, x], p_send.at[1], p_recv.at[1], cluster_peer(0, k)).start()
    some = gp.at[y, pl.ds(0, NX - 1)]
    copy(some, some, p_send.at[1], p_recv.at[1], here).wait()
    for k in range(1, NY):
        copy(gp.at[y], gp.at[y], p_send.at[2], p_recv.at[2], group_peer((y + k) % NY, core)).start()
    some = gp.at[pl.ds(0, NY - 1)]
    copy(some, some, p_send.at[2], p_recv.at[2], here).wait()

    def spread(yy, carry):
        flat = gp[yy].reshape(OWNERS * 16, 128)
        i, j = iota((POOL, OWNERS * 16), 0), iota((POOL, OWNERS * 16), 1)
        base = (i >> 5) * (NZ * 16) + (i & 15) * 16 + ((i >> 4) & 1) * 8
        for cb in range(8):
            part = jnp.dot(onehot(j == base + cb), flat, preferred_element_type=F32).astype(BF16)
            pool[:, pl.ds(pl.multiple_of(yy * W + cb * 128, 128), 128)] = part
        return carry

    lax.fori_loop(0, NY, spread, 0)

    i, j = iota((256, 256), 0), iota((256, 256), 1)
    unmix = onehot(((i >> 2) & 15) * 16 + (i >> 6) * 4 + (i & 3) == j)
    mix = onehot(((j >> 2) & 15) * 16 + (j >> 6) * 4 + (j & 3) == i)
    contract = (((1,), (1,)), ((), ()))

    def work(c, carry):
        loss_sum, scale_sum = carry
        some = rcv.at[pl.ds(c * PER, PER)]
        rows = rcv[pl.ds(c * PER, PER)].reshape(PER * 16, W)
        plain = jnp.dot(unmix, rows, preferred_element_type=F32).astype(BF16)
        for b in range(4):
            routed[pl.ds(c * SLOTS, SLOTS), b * W:(b + 1) * W] = plain[b * SLOTS:(b + 1) * SLOTS]
        mine = routed[pl.ds(c * SLOTS, SLOTS), :]
        raw_blk = lax.dot_general(mine, p_ref[...], contract, preferred_element_type=F32)
        raw_pool = lax.dot_general(mine, pool[...], contract, preferred_element_type=F32)
        expand = onehot((iota((SLOTS, PER), 0) >> 2) == iota((SLOTS, PER), 1))
        got = mrcv[pl.ds(c * PER, PER), 0, :].astype(BF16)
        got = jnp.dot(expand, got, preferred_element_type=F32)
        lanes, rank = iota((SLOTS, 128), 1), iota((SLOTS, 128), 0) & 3

        def column(f):
            return jnp.sum(jnp.where(lanes == 4 * f + rank, got, 0.0), axis=1, keepdims=True)

        first, second, place, weight = column(0), column(1), column(2), column(3)
        cand = iota((SLOTS, TP), 1)
        block = (cand >> 6).astype(F32)
        allowed = (block == first) | (block == second)
        hit = cand.astype(F32) == first * BLOCK + place
        score_blk = factor * raw_blk
        score_pool = factor * raw_pool
        peak = jnp.maximum(
            jnp.max(jnp.where(allowed, score_blk, -jnp.inf), axis=1, keepdims=True),
            jnp.max(score_pool, axis=1, keepdims=True),
        )
        exp_blk = jnp.where(allowed, jnp.exp(jnp.where(allowed, score_blk - peak, 0.0)), 0.0)
        exp_pool = jnp.exp(score_pool - peak)
        total = jnp.sum(exp_blk, axis=1, keepdims=True) + jnp.sum(exp_pool, axis=1, keepdims=True)
        log_total = peak + jnp.log(total)
        score_pos = jnp.sum(jnp.where(hit, score_blk, 0.0), axis=1, keepdims=True)
        loss_sum = loss_sum + jnp.sum(weight * (log_total - score_pos), axis=0, keepdims=True)
        grad_blk = weight * (exp_blk / total - jnp.where(hit, 1.0, 0.0))
        grad_pool = weight * (exp_pool / total)
        both = jnp.sum(grad_blk * raw_blk, axis=1, keepdims=True) + jnp.sum(grad_pool * raw_pool, axis=1, keepdims=True)
        scale_sum = scale_sum + INV_ROOT * jnp.sum(both, axis=0, keepdims=True)
        low[pl.ds(c * SLOTS, SLOTS), 0:TP] = grad_blk
        low[pl.ds(c * SLOTS, SLOTS), 256:256 + POOL] = grad_pool
        low_blk, low_pool = grad_blk.astype(BF16), grad_pool.astype(BF16)
        for b in range(4):
            cols = slice(b * W, (b + 1) * W)
            part = jnp.dot(low_blk, p_ref[:, cols], preferred_element_type=F32)
            part = part + jnp.dot(low_pool, pool[:, cols], preferred_element_type=F32)
            stack[b * SLOTS:(b + 1) * SLOTS, :] = (factor * part).astype(BF16)
        mixed = jnp.dot(mix, stack[...], preferred_element_type=F32).astype(BF16)
        gsnd[pl.ds(c * PER, PER)] = mixed.reshape(PER, 16, W)
        return loss_sum, scale_sum

    def bundles(ref, c):
        lo = 1 if c == 0 else c * PER
        return ref.at[pl.ds(lo, (c + 1) * PER - lo)]

    def owner_step(c, sums):
        some = bundles(rcv, c)
        copy(some, some, d_send, d_recv.at[c], here).wait_recv()
        some = bundles(mrcv, c)
        copy(some, some, m_send, m_recv.at[c], here).wait_recv()
        sums = work(c, sums)

        def back(o, carry):
            dz, dx = offset(o)
            copy(gsnd.at[o], grcv.at[o], g_send, g_recv.at[o // PER], cluster_peer(-dz, -dx)).start()
            return carry

        lax.fori_loop(1 if c == 0 else c * PER, (c + 1) * PER, back, 0)
        return sums

    sums = (jnp.zeros((1, 1), F32), jnp.zeros((1, 1), F32))
    for c in range(CHUNKS):
        sums = owner_step(c, sums)
    grcv[0] = gsnd[0]

    low[:, TP:256] = jnp.zeros((256, 256 - TP), F32)
    lowt[...] = low[...].T.astype(BF16)

    def pool_term(k, carry):
        cols = pl.ds(pl.multiple_of(k * 512, 512), 512)
        part = jnp.dot(lowt[256:256 + POOL, :], routed[:, cols], preferred_element_type=F32)
        pt[k % 2, k // 2] = factor * part
        return carry

    lax.fori_loop(0, 8, pool_term, 0)
    tile_lane = iota((8, 128), 1)
    sc[0] = jnp.where(tile_lane == 0, sums[0], jnp.where(tile_lane == 1, sums[1], 0.0))

    peer = group_peer(y, 1 - core)
    move = [
        copy(pt.at[1 - core], rc, r_send.at[0], r_recv.at[0], peer),
        copy(sc.at[0], rcs, t_send.at[0], t_recv.at[0], peer),
    ]
    for one in move:
        one.start()

    def passage_term(k, carry):
        cols = pl.ds(pl.multiple_of(k * 512, 512), 512)
        part = jnp.dot(lowt[0:TP, :], routed[:, cols], preferred_element_type=F32)
        pg_ref[:, cols] = (factor * part).astype(BF16)
        return carry

    lax.fori_loop(0, 8, passage_term, 0)
    for one in move:
        one.wait()
    s1[...] = pt[core] + rc[...]
    sc[1] = sc[0] + rcs[...]

    for k in range(1, NY):
        to = (y + k) % NY
        copy(s1.at[to], ry.at[k - 1], r_send.at[1], r_recv.at[1], group_peer(to, core)).start()
        copy(sc.at[1], rys.at[k - 1], t_send.at[1], t_recv.at[1], group_peer(to, core)).start()
    copy(ry, ry, r_send.at[1], r_recv.at[1], here).wait()
    copy(rys, rys, t_send.at[1], t_recv.at[1], here).wait()
    s2[...] = (s1[y] + ry[0] + ry[1] + ry[2]).reshape(NX, 32, 512)
    sc[2] = sc[1] + rys[0] + rys[1] + rys[2]

    for k in range(1, NX):
        to = (x + k) % NX
        copy(s2.at[to], rx.at[k - 1], r_send.at[2], r_recv.at[2], cluster_peer(0, k)).start()
        copy(sc.at[2], rxs.at[k - 1], t_send.at[2], t_recv.at[2], cluster_peer(0, k)).start()
    copy(rx, rx, r_send.at[2], r_recv.at[2], here).wait()
    copy(rxs, rxs, t_send.at[2], t_recv.at[2], here).wait()
    s3 = s2[x] + rx[0] + rx[1] + rx[2]
    scalars = sc[2] + rxs[0] + rxs[1] + rxs[2]
    for r in range(2):
        for cb in range(4):
            zb[:, r * 4 + cb, :] = s3[r * NZ:(r + 1) * NZ, cb * 128:(cb + 1) * 128]
    zb[:, 8:16, :] = jnp.broadcast_to(scalars[None], (NZ, 8, 128))

    def to_z(k, carry):
        copy(zb.at[(z + k) % NZ], rz.at[k - 1], r_send.at[3], r_recv.at[3], cluster_peer(k, 0)).start()
        return carry

    lax.fori_loop(1, NZ, to_z, 0)
    copy(rz, rz, r_send.at[3], r_recv.at[3], here).wait()
    last = zb[z] + jnp.sum(rz[...], axis=0)
    fin[...] = last[0:8]
    gb[grp] = last[0:8]
    loss_ref[0] = jnp.sum(jnp.where(tile_lane[0:1] == 0, last[8:9], 0.0)) * (1.0 / (TQ * OWNERS * 8))
    sgrad_ref[0] = jnp.sum(jnp.where(tile_lane[0:1] == 1, last[8:9], 0.0))

    def to_group(k, carry):
        copy(fin, gb.at[grp], r_send.at[4], r_recv.at[4], ((grp + k) % 8, clu)).start()
        return carry

    lax.fori_loop(1, 8, to_group, 0)

    def take(c):
        some = bundles(grcv, c)
        copy(some, some, g_send, g_recv.at[c], here).wait_recv()
        rows = grcv[pl.ds(c * PER, PER)].reshape(PER * 16, W)
        lanes = iota((TQ, PER * 16), 1) + c * (PER * 16)
        for b in range(4):
            part = jnp.dot(onehot(lanes == place_col + 4 * b), rows, preferred_element_type=F32)
            if c == 0:
                acc[:, b * W:(b + 1) * W] = part
            elif c + 1 < CHUNKS:
                acc[:, b * W:(b + 1) * W] += part
            else:
                home_ref[:, b * W:(b + 1) * W] = (acc[:, b * W:(b + 1) * W] + part).astype(BF16)

    for c in range(CHUNKS):
        take(c)

    some = gb.at[pl.ds(0, 7)]
    copy(some, some, r_send.at[4], r_recv.at[4], here).wait()
    for g in range(8):
        for r in range(2):
            for cb in range(4):
                col = g * 512 + cb * 128
                poolg_ref[r:r + 1, col:col + 128] = gb[g, r * 4 + cb:r * 4 + cb + 1, :]

    some = rcv.at[pl.ds(1, OWNERS - 1)]
    copy(some, some, d_send, d_recv.at[0], here).wait_send()
    copy(some, some, g_send, g_recv.at[0], here).wait_send()
    some = mrcv.at[pl.ds(1, OWNERS - 1)]
    copy(some, some, m_send, m_recv.at[0], here).wait_send()


BASE = 2
V = D // 8
SPARE = 12
RING = 4 * SPARE
LATE = 2 * NZ


def fast_kernel(
    q_ref, cl_ref, bl_ref, pos_ref, p_ref, piece_ref, scale_ref,
    home_ref, pg_ref, poolg_ref, loss_ref, sgrad_ref, flag_ref,
    snd, rcv, msnd, mrcv, gsnd, grcv, stack, routed, low, lowt, acc, gp, pool,
    og, tg, px, pv, pts, ptr, rsn, rv, cc, rr, ll, late,
    pt, rc, s1, ry, s2, rx, zb, rz, fin, gb, sc, rcs, rys, rxs,
    d_send, d_recv, m_send, m_recv, g_send, g_recv, p_send, p_recv, r_send, r_recv, t_send, t_recv,
    f_send, fr_recv, fl_recv, b_send, br_recv, bl_recv, x_send, x_recv,
):
    grp = lax.axis_index("group")
    clu = lax.axis_index("cluster")
    y, core = grp // 2, grp % 2
    z, x = clu // NX, clu % NX

    def cluster_peer(dz, dx):
        return (grp, ((z + dz + NZ) % NZ) * NX + (x + dx + NX) % NX)

    def group_peer(py, pc):
        return (py * 2 + pc, clu)

    def offset(o):
        return ((o // 4) % 4) * 4 + o // 16, o % 4

    def copy(src, dst, send, recv, peer):
        return pltpu.make_async_remote_copy(
            src_ref=src, dst_ref=dst, send_sem=send, recv_sem=recv, device_id=peer, device_id_type=MESH
        )

    here = (grp, clu)
    barrier = pltpu.get_barrier_semaphore()

    def greet(o, carry):
        dz, dx = offset(o)
        pl.semaphore_signal(barrier, inc=1, device_id=cluster_peer(dz, dx), device_id_type=MESH)
        return carry

    lax.fori_loop(1, OWNERS, greet, 0)

    def greet_group(k, carry):
        pl.semaphore_signal(barrier, inc=1, device_id=((grp + k) % 8, clu), device_id_type=MESH)
        return carry

    lax.fori_loop(1, 8, greet_group, 0)

    factor = scale_ref[0] * INV_ROOT

    a_iota, b_iota = iota((TQ, TQ), 0), iota((TQ, TQ), 1)
    eye = a_iota == b_iota

    def to_col(row):
        return jnp.sum(jnp.where(eye, row.astype(F32), 0.0), axis=1, keepdims=True)

    cl_row = cl_ref[...]
    cl_col = to_col(cl_row).astype(jnp.int32)
    same = cl_col == cl_row
    rank_row = jnp.sum(jnp.where(same & (a_iota < b_iota), 1.0, 0.0), axis=0, keepdims=True).astype(jnp.int32)
    rank_col = jnp.sum(jnp.where(same & (b_iota < a_iota), 1.0, 0.0), axis=1, keepdims=True).astype(jnp.int32)
    extra_row, extra_col = rank_row >= BASE, rank_col >= BASE
    spare_row = jnp.sum(jnp.where(extra_col & (a_iota < b_iota), 1.0, 0.0), axis=0, keepdims=True).astype(jnp.int32)
    spare_col = jnp.sum(jnp.where(extra_row & (b_iota < a_iota), 1.0, 0.0), axis=1, keepdims=True).astype(jnp.int32)
    fits_row, fits_col = extra_row & (spare_row < SPARE), extra_col & (spare_col < SPARE)
    spare_row = jnp.where(fits_row, spare_row, -4096)
    spare_col = jnp.where(fits_col, spare_col, -4096)
    left_over = jnp.sum(jnp.where(extra_col & jnp.logical_not(fits_col), 1.0, 0.0), axis=0, keepdims=True)

    def offset_of(cl):
        dz = ((cl >> 2) - z) & 15
        return (dz & 3) * 16 + (dz >> 2) * 4 + ((cl - x) & 3)

    off_row, off_col = offset_of(cl_row), offset_of(cl_col)
    place_row = jnp.where(extra_row, -4096, off_row * 16 + rank_row)
    place_col = jnp.where(extra_col, -4096, off_col * 16 + rank_col)

    lane = iota((TQ, 128), 1)
    field = lane >> 2
    block0, block1, position = to_col(bl_ref[0:1, :]), to_col(bl_ref[1:2, :]), to_col(pos_ref[...])
    value = jnp.where(field == 0, block0, jnp.where(field == 1, block1, jnp.where(field == 2, position, 1.0)))
    value = jnp.where((rank_col == (lane & 3)) & (field < 4) & jnp.logical_not(extra_col), value, 0.0).astype(BF16)
    meta = jnp.dot(onehot(iota((OWNERS, TQ), 0) == off_row), value, preferred_element_type=F32)
    msnd[:, 0, :] = meta

    total = jnp.zeros((RING, W), F32)
    for b in range(4):
        pick = onehot(iota((RING, TQ), 0) == spare_row + SPARE * b)
        total = total + jnp.dot(pick, q_ref[:, b * W:(b + 1) * W], preferred_element_type=F32)
    og[z] = total.astype(BF16)
    kind = iota((8, TQ), 0)
    facts = jnp.where(
        kind == 0, cl_row.astype(F32),
        jnp.where(
            kind == 1, bl_ref[0:1, :].astype(F32),
            jnp.where(kind == 2, bl_ref[1:2, :].astype(F32), jnp.where(kind == 3, pos_ref[...].astype(F32), 1.0)),
        ),
    )
    facts = jnp.where(kind < 5, facts, 0.0).astype(BF16)
    spot = lane % SPARE
    tg[z] = jnp.dot(facts, onehot((spot == spare_col) & (lane < RING)), preferred_element_type=F32)

    def build(c):
        row = iota((PER * 16, TQ), 0) + c * (PER * 16)
        total = jnp.zeros((PER * 16, V), F32)
        for b in range(8):
            pick = onehot(row == place_row + BASE * b)
            total = total + jnp.dot(pick, q_ref[:, b * V:(b + 1) * V], preferred_element_type=F32)
        snd[pl.ds(c * PER, PER)] = total.astype(BF16).reshape(PER, 16, V)

    EIGHT = OWNERS // 8

    def send(e):
        def step(o, carry):
            dz, dx = offset(o)
            peer = cluster_peer(dz, dx)
            copy(msnd.at[o], mrcv.at[o], m_send, m_recv.at[o // PER], peer).start()
            copy(snd.at[o], rcv.at[o], d_send, d_recv.at[o // PER], peer).start()
            return carry

        lax.fori_loop(1 if e == 0 else e * EIGHT, (e + 1) * EIGHT, step, 0)

    def right(k):
        one = og.at[(z - k + 1 + NZ) % NZ]
        return copy(one, one, f_send.at[0], fr_recv.at[k - 1], cluster_peer(1, 0))

    def left(k):
        one = og.at[(z + k - 1) % NZ]
        return copy(one, one, f_send.at[1], fl_recv.at[k - 1], cluster_peer(-1, 0))

    def ring(k):
        if k > 1:
            one = og.at[(z - k + 1 + NZ) % NZ]
            copy(one, one, f_send.at[0], fr_recv.at[k - 2], here).wait_recv()
            one = og.at[(z + k - 1) % NZ]
            copy(one, one, f_send.at[1], fl_recv.at[k - 2], here).wait_recv()
        right(k).start()
        if k < 8:
            left(k).start()

    def spread():
        i, j = iota((8 * POOL, OWNERS * 16), 0), iota((8 * POOL, OWNERS * 16), 1)
        at = i & 127
        order = onehot(j == (at >> 5) * (NZ * 16) + (at & 15) * 16 + ((at >> 4) & 1) * 8 + (i >> 7))
        for pair in range(2):
            flat = jnp.concatenate(
                [gp[2 * pair].reshape(OWNERS * 16, 128), gp[2 * pair + 1].reshape(OWNERS * 16, 128)], axis=1
            )
            part = jnp.dot(order, flat, preferred_element_type=F32).astype(BF16)
            for cb in range(8):
                for one in range(2):
                    col = (2 * pair + one) * W + cb * 128
                    pool[:, col:col + 128] = part[cb * 128:(cb + 1) * 128, one * 128:(one + 1) * 128]

    def gather_facts(k, carry):
        source = iota((128, NZ * RING), 0)
        shift = onehot((iota((128, NZ * RING), 1) == source + k * RING) & (source < RING))
        return carry + jnp.dot(tg[k].astype(BF16), shift, preferred_element_type=F32)

    gp[y, x, z] = piece_ref[y]
    build(0)
    build(1)
    pl.semaphore_wait(barrier, OWNERS - 1 + 7)
    ring(1)

    def early(k, carry):
        copy(tg.at[z], tg.at[z], t_send.at[3], t_recv.at[3], cluster_peer(k, 0)).start()
        copy(gp.at[y, x, z], gp.at[y, x, z], p_send.at[0], p_recv.at[0], cluster_peer(k, 0)).start()
        return carry

    lax.fori_loop(1, NZ, early, 0)
    send(0)
    ring(2)
    send(1)
    build(2)
    ring(3)
    send(2)
    some = gp.at[y, x, pl.ds(0, NZ - 1)]
    copy(some, some, p_send.at[0], p_recv.at[0], here).wait()
    for k in range(1, NX):
        copy(gp.at[y, x], gp.at[y, x], p_send.at[1], p_recv.at[1], cluster_peer(0, k)).start()
    build(3)
    ring(4)
    send(3)

    some = tg.at[pl.ds(0, NZ - 1)]
    copy(some, some, t_send.at[3], t_recv.at[3], here).wait()
    span = NZ * RING
    known = lax.fori_loop(0, NZ // 2, gather_facts, jnp.zeros((8, span), F32))
    ring(5)
    send(4)
    known = lax.fori_loop(NZ // 2, NZ, gather_facts, known)
    some = gp.at[y, pl.ds(0, NX - 1)]
    copy(some, some, p_send.at[1], p_recv.at[1], here).wait()
    for k in range(1, NY):
        copy(gp.at[y], gp.at[y], p_send.at[2], p_recv.at[2], group_peer((y + k) % NY, core)).start()
    ring(6)
    dest = known[0:1].astype(jnp.int32)
    local = (known[4:5] > 0.5) & ((dest >> 2) == z)
    across = iota((1, span), 1)
    block_of = (across % RING) // SPARE
    to_x = dest & 3
    mark = (iota((8, span), 0) == to_x) & local & (block_of == 0)
    before = onehot(iota((span, span), 0) < across - block_of * SPARE)
    ranks = jnp.dot(onehot(mark), before, preferred_element_type=F32)
    order = jnp.sum(jnp.where(iota((8, span), 0) == to_x, ranks, 0.0), axis=0, keepdims=True).astype(jnp.int32)
    ring(7)
    key = jnp.where(local, to_x * (4 * LATE) + block_of * LATE + order, -1)
    first_key = jnp.where(local & (block_of == 0), to_x * LATE + order, -1)
    key_col = jnp.broadcast_to(key.astype(F32), (8, span)).T[:, 0:1].astype(jnp.int32)
    pts[...] = lax.dot_general(
        known.astype(BF16), onehot(iota((NX * LATE, span), 0) == first_key), (((1,), (1,)), ((), ())),
        preferred_element_type=F32,
    )
    ring(8)
    rcv[0] = snd[0]
    mrcv[0] = msnd[0]
    one = og.at[(z + 8) % NZ]
    copy(one, one, f_send.at[0], fr_recv.at[7], here).wait_recv()
    send(5)
    send(6)
    send(7)
    pick = onehot(iota((NX * 4 * LATE, span), 0) == key)
    for ct in range(4):
        cols = slice(ct * 256, (ct + 1) * 256)
        part = jnp.dot(pick, og[:, :, cols].reshape(span, 256), preferred_element_type=F32).astype(BF16)
        px[:, :, cols] = part.reshape(NX, 4 * LATE, 256)
    for k in range(1, NX):
        copy(px.at[(x + k) % NX], pv.at[x], x_send.at[0], x_recv.at[0], cluster_peer(0, k)).start()
        copy(pts, ptr.at[x], x_send.at[1], x_recv.at[1], cluster_peer(0, k)).start()
    pv[x] = px[x]
    ptr[x] = pts[...]
    some = gp.at[pl.ds(0, NY - 1)]
    copy(some, some, p_send.at[2], p_recv.at[2], here).wait()
    spread()

    i, j = iota((256, 256), 0), iota((256, 256), 1)
    unmix = onehot(((i >> 1) & 15) * 16 + (i >> 5) * 2 + (i & 1) == j)
    mix = onehot(((j >> 1) & 15) * 16 + (j >> 5) * 2 + (j & 1) == i)
    contract = (((1,), (1,)), ((), ()))

    def work(lo, count, columns, sums):
        loss_sum, scale_sum = sums
        first, second, place, weight = columns
        mine = routed[lo:lo + count, :]
        raw_blk = lax.dot_general(mine, p_ref[...], contract, preferred_element_type=F32)
        raw_pool = lax.dot_general(mine, pool[...], contract, preferred_element_type=F32)
        cand = iota((count, TP), 1)
        block = (cand >> 6).astype(F32)
        allowed = (block == first) | (block == second)
        hit = cand.astype(F32) == first * BLOCK + place
        score_blk = factor * raw_blk
        score_pool = factor * raw_pool
        peak = jnp.maximum(
            jnp.max(jnp.where(allowed, score_blk, -jnp.inf), axis=1, keepdims=True),
            jnp.max(score_pool, axis=1, keepdims=True),
        )
        exp_blk = jnp.where(allowed, jnp.exp(jnp.where(allowed, score_blk - peak, 0.0)), 0.0)
        exp_pool = jnp.exp(score_pool - peak)
        total = jnp.sum(exp_blk, axis=1, keepdims=True) + jnp.sum(exp_pool, axis=1, keepdims=True)
        log_total = peak + jnp.log(total)
        score_pos = jnp.sum(jnp.where(hit, score_blk, 0.0), axis=1, keepdims=True)
        loss_sum = loss_sum + jnp.sum(weight * (log_total - score_pos), axis=0, keepdims=True)
        grad_blk = weight * (exp_blk / total - jnp.where(hit, 1.0, 0.0))
        grad_pool = weight * (exp_pool / total)
        both = jnp.sum(grad_blk * raw_blk, axis=1, keepdims=True) + jnp.sum(grad_pool * raw_pool, axis=1, keepdims=True)
        scale_sum = scale_sum + INV_ROOT * jnp.sum(both, axis=0, keepdims=True)
        low[lo:lo + count, 0:TP] = grad_blk
        low[lo:lo + count, 256:256 + POOL] = grad_pool
        low_blk, low_pool = grad_blk.astype(BF16), grad_pool.astype(BF16)

        def grads(cols):
            part = jnp.dot(low_blk, p_ref[:, cols], preferred_element_type=F32)
            part = part + jnp.dot(low_pool, pool[:, cols], preferred_element_type=F32)
            return (factor * part).astype(BF16)

        return (loss_sum, scale_sum), grads

    def bundles(ref, c):
        lo = 1 if c == 0 else c * PER
        return ref.at[pl.ds(lo, (c + 1) * PER - lo)]

    HALF = 2 * PER * BASE

    def half(h, sums):
        for c in (2 * h, 2 * h + 1):
            some = bundles(rcv, c)
            copy(some, some, d_send, d_recv.at[c], here).wait_recv()
            some = bundles(mrcv, c)
            copy(some, some, m_send, m_recv.at[c], here).wait_recv()
            rows = rcv[pl.ds(c * PER, PER)].reshape(PER * 16, V)
            plain = jnp.dot(unmix, rows, preferred_element_type=F32).astype(BF16)
            for b in range(8):
                routed[c * 32:(c + 1) * 32, b * V:(b + 1) * V] = plain[b * 32:(b + 1) * 32]
        expand = onehot((iota((HALF, 2 * PER), 0) >> 1) == iota((HALF, 2 * PER), 1))
        got = mrcv[pl.ds(2 * h * PER, 2 * PER), 0, :].astype(BF16)
        got = jnp.dot(expand, got, preferred_element_type=F32)
        lanes, rank = iota((HALF, 128), 1), iota((HALF, 128), 0) & 1

        def column(f):
            return jnp.sum(jnp.where(lanes == 4 * f + rank, got, 0.0), axis=1, keepdims=True)

        sums, grads = work(h * HALF, HALF, [column(f) for f in range(4)], sums)
        for b in range(8):
            part = grads(slice(b * V, (b + 1) * V))
            stack[0, b * 32:(b + 1) * 32, :] = part[0:32]
            stack[1, b * 32:(b + 1) * 32, :] = part[32:64]
        for c in (0, 1):
            mixed = jnp.dot(mix, stack[c], preferred_element_type=F32).astype(BF16)
            gsnd[pl.ds((2 * h + c) * PER, PER)] = mixed.reshape(PER, 16, V)
        return sums

    def send_back(e):
        def back(o, carry):
            dz, dx = offset(o)
            copy(gsnd.at[o], grcv.at[o], g_send, g_recv.at[o // PER], cluster_peer(-dz, -dx)).start()
            return carry

        lax.fori_loop(1 if e == 0 else e * EIGHT, (e + 1) * EIGHT, back, 0)

    sums = (jnp.zeros((1, 1), F32), jnp.zeros((1, 1), F32))
    sums = half(0, sums)
    for e in range(4):
        send_back(e)
    grcv[0] = gsnd[0]

    some = pv.at[pl.ds(0, NX - 1)]
    copy(some, some, x_send.at[0], x_recv.at[0], here).wait()
    some = ptr.at[pl.ds(0, NX - 1)]
    copy(some, some, x_send.at[1], x_recv.at[1], here).wait()
    choose = onehot(iota((LATE, 128), 1) == iota((LATE, 128), 0) + x * LATE)
    for via in range(NX):
        for b in range(4):
            routed[128 + via * LATE:128 + (via + 1) * LATE, b * W:(b + 1) * W] = pv[via, b * LATE:(b + 1) * LATE, :]
        late[via * LATE:(via + 1) * LATE, 0:8] = lax.dot_general(
            choose, ptr[via].astype(BF16), contract, preferred_element_type=F32
        )
    sums, grads = work(128, 128, [late[:, f:f + 1] for f in range(1, 5)], sums)
    for b in range(4):
        part = grads(slice(b * W, (b + 1) * W))
        for via in range(NX):
            rsn[via, b * LATE:(b + 1) * LATE, :] = part[via * LATE:(via + 1) * LATE]
    for k in range(1, NX):
        copy(rsn.at[(x + k) % NX], rv.at[x], x_send.at[2], x_recv.at[2], cluster_peer(0, k)).start()
    rv[x] = rsn[x]

    some = rv.at[pl.ds(0, NX - 1)]
    copy(some, some, x_send.at[2], x_recv.at[2], here).wait()
    pick = onehot(iota((span, NX * 4 * LATE), 1) == key_col)
    for ct in range(4):
        cols = slice(ct * 256, (ct + 1) * 256)
        part = jnp.dot(pick, rv[:, :, cols].reshape(NX * 4 * LATE, 256), preferred_element_type=F32).astype(BF16)
        cc[:, :, cols] = part.reshape(NZ, RING, 256)

    def ring_back(k):
        to = (z + 9 - k) % NZ
        if k > 1:
            copy(rr.at[k - 2], rr.at[k - 2], b_send.at[0], br_recv.at[k - 2], here).wait_recv()
            cc[to] = cc[to] + rr[k - 2]
        copy(cc.at[to], rr.at[k - 1], b_send.at[0], br_recv.at[k - 1], cluster_peer(1, 0)).start()
        if k < 8:
            to = (z - 8 + k + NZ) % NZ
            if k > 1:
                copy(ll.at[k - 2], ll.at[k - 2], b_send.at[1], bl_recv.at[k - 2], here).wait_recv()
                cc[to] = cc[to] + ll[k - 2]
            copy(cc.at[to], ll.at[k - 1], b_send.at[1], bl_recv.at[k - 1], cluster_peer(-1, 0)).start()

    ring_back(1)
    sums = half(1, sums)
    ring_back(2)
    send_back(4)

    low[:, TP:256] = jnp.zeros((256, 256 - TP), F32)
    lowt[...] = low[...].T.astype(BF16)

    def pool_term(k, carry):
        cols = pl.ds(pl.multiple_of(k * 512, 512), 512)
        part = jnp.dot(lowt[256:256 + POOL, :], routed[:, cols], preferred_element_type=F32)
        pt[k % 2, k // 2] = factor * part
        return carry

    lax.fori_loop(0, 8, pool_term, 0)
    tile_lane = iota((8, 128), 1)
    sc[0] = jnp.where(
        tile_lane == 0, sums[0], jnp.where(tile_lane == 1, sums[1], jnp.where(tile_lane == 2, left_over, 0.0))
    )

    peer = group_peer(y, 1 - core)
    move = [
        copy(pt.at[1 - core], rc, r_send.at[0], r_recv.at[0], peer),
        copy(sc.at[0], rcs, t_send.at[0], t_recv.at[0], peer),
    ]
    for one in move:
        one.start()
    ring_back(3)
    send_back(5)

    def passage_term(k, carry):
        cols = pl.ds(pl.multiple_of(k * 512, 512), 512)
        part = jnp.dot(lowt[0:TP, :], routed[:, cols], preferred_element_type=F32)
        pg_ref[:, cols] = (factor * part).astype(BF16)
        return carry

    lax.fori_loop(0, 4, passage_term, 0)
    ring_back(4)
    send_back(6)
    lax.fori_loop(4, 8, passage_term, 0)
    for one in move:
        one.wait()
    s1[...] = pt[core] + rc[...]
    sc[1] = sc[0] + rcs[...]

    for k in range(1, NY):
        to = (y + k) % NY
        copy(s1.at[to], ry.at[k - 1], r_send.at[1], r_recv.at[1], group_peer(to, core)).start()
        copy(sc.at[1], rys.at[k - 1], t_send.at[1], t_recv.at[1], group_peer(to, core)).start()
    ring_back(5)
    send_back(7)
    copy(ry, ry, r_send.at[1], r_recv.at[1], here).wait()
    copy(rys, rys, t_send.at[1], t_recv.at[1], here).wait()
    s2[...] = (s1[y] + ry[0] + ry[1] + ry[2]).reshape(NX, 32, 512)
    sc[2] = sc[1] + rys[0] + rys[1] + rys[2]

    for k in range(1, NX):
        to = (x + k) % NX
        copy(s2.at[to], rx.at[k - 1], r_send.at[2], r_recv.at[2], cluster_peer(0, k)).start()
        copy(sc.at[2], rxs.at[k - 1], t_send.at[2], t_recv.at[2], cluster_peer(0, k)).start()
    ring_back(6)
    copy(rx, rx, r_send.at[2], r_recv.at[2], here).wait()
    copy(rxs, rxs, t_send.at[2], t_recv.at[2], here).wait()
    s3 = s2[x] + rx[0] + rx[1] + rx[2]
    scalars = sc[2] + rxs[0] + rxs[1] + rxs[2]
    for r in range(2):
        for cb in range(4):
            zb[:, r * 4 + cb, :] = s3[r * NZ:(r + 1) * NZ, cb * 128:(cb + 1) * 128]
    zb[:, 8:16, :] = jnp.broadcast_to(scalars[None], (NZ, 8, 128))

    def to_z(k, carry):
        copy(zb.at[(z + k) % NZ], rz.at[k - 1], r_send.at[3], r_recv.at[3], cluster_peer(k, 0)).start()
        return carry

    lax.fori_loop(1, NZ, to_z, 0)
    ring_back(7)
    copy(rz, rz, r_send.at[3], r_recv.at[3], here).wait()
    last = zb[z] + jnp.sum(rz[...], axis=0)
    fin[...] = last[0:8]
    gb[grp] = last[0:8]
    loss_ref[0] = jnp.sum(jnp.where(tile_lane[0:1] == 0, last[8:9], 0.0)) * (1.0 / (TQ * OWNERS * 8))
    sgrad_ref[0] = jnp.sum(jnp.where(tile_lane[0:1] == 1, last[8:9], 0.0))
    flag_ref[0] = jnp.sum(jnp.where(tile_lane[0:1] == 2, last[8:9], 0.0))

    def to_group(k, carry):
        copy(fin, gb.at[grp], r_send.at[4], r_recv.at[4], ((grp + k) % 8, clu)).start()
        return carry

    lax.fori_loop(1, 8, to_group, 0)
    ring_back(8)

    def take(c):
        some = bundles(grcv, c)
        copy(some, some, g_send, g_recv.at[c], here).wait_recv()
        rows = grcv[pl.ds(c * PER, PER)].reshape(PER * 16, V)
        lanes = iota((TQ, PER * 16), 1) + c * (PER * 16)
        pick = jnp.concatenate([onehot(lanes == place_col + BASE * b) for b in range(8)], axis=0)
        part = jnp.dot(pick, rows, preferred_element_type=F32)
        for b in range(8):
            if c == 0:
                acc[:, b * V:(b + 1) * V] = part[b * TQ:(b + 1) * TQ]
            else:
                acc[:, b * V:(b + 1) * V] += part[b * TQ:(b + 1) * TQ]

    for c in range(CHUNKS):
        take(c)
    copy(rr.at[7], rr.at[7], b_send.at[0], br_recv.at[7], here).wait_recv()
    copy(ll.at[6], ll.at[6], b_send.at[1], bl_recv.at[6], here).wait_recv()
    spare_rows = cc[z] + rr[7] + ll[6]
    for b in range(4):
        pick = onehot(iota((TQ, RING), 1) == spare_col + SPARE * b)
        part = jnp.dot(pick, spare_rows, preferred_element_type=F32)
        home_ref[:, b * W:(b + 1) * W] = (acc[:, b * W:(b + 1) * W] + part).astype(BF16)

    some = gb.at[pl.ds(0, 7)]
    copy(some, some, r_send.at[4], r_recv.at[4], here).wait()
    for g in range(8):
        for r in range(2):
            for cb in range(4):
                col = g * 512 + cb * 128
                poolg_ref[r:r + 1, col:col + 128] = gb[g, r * 4 + cb:r * 4 + cb + 1, :]

    some = rcv.at[pl.ds(1, OWNERS - 1)]
    copy(some, some, d_send, d_recv.at[0], here).wait_send()
    copy(some, some, g_send, g_recv.at[0], here).wait_send()
    some = mrcv.at[pl.ds(1, OWNERS - 1)]
    copy(some, some, m_send, m_recv.at[0], here).wait_send()
    for side, count in ((0, 8), (1, 7)):
        some = og.at[pl.ds(0, count)]
        copy(some, some, f_send.at[side], fr_recv.at[0], here).wait_send()
        some = cc.at[pl.ds(0, count)]
        copy(some, some, b_send.at[side], br_recv.at[0], here).wait_send()


def reduce_scratch():
    return [
        pltpu.VMEM((2, NY, POOL, 512), F32),
        pltpu.VMEM((NY, POOL, 512), F32),
        pltpu.VMEM((NY, POOL, 512), F32),
        pltpu.VMEM((NY - 1, POOL, 512), F32),
        pltpu.VMEM((NX, 32, 512), F32),
        pltpu.VMEM((NX - 1, 32, 512), F32),
        pltpu.VMEM((NZ, 16, 128), F32),
        pltpu.VMEM((NZ - 1, 16, 128), F32),
        pltpu.VMEM((8, 128), F32),
        pltpu.VMEM((8, 8, 128), F32),
        pltpu.VMEM((3, 8, 128), F32),
        pltpu.VMEM((8, 128), F32),
        pltpu.VMEM((NY - 1, 8, 128), F32),
        pltpu.VMEM((NX - 1, 8, 128), F32),
    ]


def fast_call(*args):
    vm = pl.BlockSpec(memory_space=pltpu.VMEM)
    sm = pl.BlockSpec(memory_space=pltpu.SMEM)
    bundle = pltpu.VMEM((OWNERS, 16, V), BF16)
    note = pltpu.VMEM((OWNERS, 1, 128), F32)
    column = pltpu.VMEM((NX, 4 * LATE, W), BF16)
    dma = pltpu.SemaphoreType.DMA
    scalar = jax.ShapeDtypeStruct((1,), F32)
    return pl.pallas_call(
        fast_kernel,
        out_shape=(
            jax.ShapeDtypeStruct((TQ, D), BF16),
            jax.ShapeDtypeStruct((TP, D), BF16),
            jax.ShapeDtypeStruct((2, D), F32),
            scalar, scalar, scalar,
        ),
        in_specs=[vm] * 6 + [sm],
        out_specs=(vm, vm, vm, sm, sm, sm),
        scratch_shapes=[
            bundle, bundle, note, note, bundle, bundle,
            pltpu.VMEM((2, 256, V), BF16),
            pltpu.VMEM((256, D), BF16),
            pltpu.VMEM((256, 384), F32),
            pltpu.VMEM((384, 256), BF16),
            pltpu.VMEM((TQ, D), F32),
            pltpu.VMEM((NY, NX, NZ, 16, 128), BF16),
            pltpu.VMEM((POOL, D), BF16),
            pltpu.VMEM((NZ, RING, W), BF16),
            pltpu.VMEM((NZ, 8, 128), F32),
            column, column,
            pltpu.VMEM((8, 128), F32),
            pltpu.VMEM((NX, 8, 128), F32),
            column, column,
            pltpu.VMEM((NZ, RING, W), BF16),
            pltpu.VMEM((8, RING, W), BF16),
            pltpu.VMEM((7, RING, W), BF16),
            pltpu.VMEM((128, 128), F32),
            *reduce_scratch(),
            dma, dma((CHUNKS,)), dma, dma((CHUNKS,)), dma, dma((CHUNKS,)),
            dma((3,)), dma((3,)), dma((5,)), dma((5,)), dma((4,)), dma((4,)),
            dma((2,)), dma((8,)), dma((7,)), dma((2,)), dma((8,)), dma((7,)), dma((3,)), dma((3,)),
        ],
        compiler_params=pltpu.CompilerParams(
            collective_id=1, has_side_effects=True, vmem_limit_bytes=48 * 1024 * 1024
        ),
        cost_estimate=pl.CostEstimate(flops=4 * 10**9, bytes_accessed=6 * 10**6, transcendentals=82000),
    )(*args)


def full_call(*args):
    vm = pl.BlockSpec(memory_space=pltpu.VMEM)
    sm = pl.BlockSpec(memory_space=pltpu.SMEM)
    bundle = pltpu.VMEM((OWNERS, 16, W), BF16)
    note = pltpu.VMEM((OWNERS, 1, 128), F32)
    dma = pltpu.SemaphoreType.DMA
    return pl.pallas_call(
        full_kernel,
        out_shape=(
            jax.ShapeDtypeStruct((TQ, D), BF16),
            jax.ShapeDtypeStruct((TP, D), BF16),
            jax.ShapeDtypeStruct((2, D), F32),
            jax.ShapeDtypeStruct((1,), F32),
            jax.ShapeDtypeStruct((1,), F32),
        ),
        in_specs=[vm] * 6 + [sm],
        out_specs=(vm, vm, vm, sm, sm),
        scratch_shapes=[
            bundle, bundle, note, note, bundle, bundle,
            pltpu.VMEM((256, W), BF16),
            pltpu.VMEM((256, D), BF16),
            pltpu.VMEM((256, 384), F32),
            pltpu.VMEM((384, 256), BF16),
            pltpu.VMEM((TQ, D), F32),
            pltpu.VMEM((NY, NX, NZ, 16, 128), BF16),
            pltpu.VMEM((POOL, D), BF16),
            *reduce_scratch(),
            dma, dma((CHUNKS,)), dma, dma((CHUNKS,)), dma, dma((CHUNKS,)),
            dma((3,)), dma((3,)), dma((5,)), dma((5,)), dma((3,)), dma((3,)),
        ],
        compiler_params=pltpu.CompilerParams(
            collective_id=0, has_side_effects=True, vmem_limit_bytes=48 * 1024 * 1024
        ),
        cost_estimate=pl.CostEstimate(flops=4 * 10**9, bytes_accessed=6 * 10**6, transcendentals=82000),
    )(*args)


def per_device(queries, cluster_id, block_list, positive, passages, pool_rows, logit_scale):
    piece = pool_rows.reshape(2, 4, 8, 128).transpose(1, 0, 2, 3).reshape(4, 16, 128)
    args = (
        queries,
        cluster_id.reshape(1, TQ),
        block_list.T,
        positive.reshape(1, TQ),
        passages,
        piece,
        logit_scale,
    )
    *quick, left_over = fast_call(*args)
    return lax.cond(left_over[0] > 0.5, lambda: tuple(full_call(*args)), lambda: tuple(quick))


def solution(mesh):
    placed = (
        P(("group", "cluster"), None),
        P(("group", "cluster"), None),
        P(("group", "cluster"), None),
        P(("group", "cluster")),
        P(("group", "cluster"), None),
        P("cluster", None),
        P(),
    )
    return jax.shard_map(
        per_device,
        mesh=mesh,
        in_specs=placed,
        out_specs=(
            P(("group", "cluster"), None),
            P(("group", "cluster"), None),
            P("cluster", None),
            P(),
            P(),
        ),
        check_vma=False,
    )
```

```python
import math

import jax
import jax.numpy as jnp
from jax import lax
from jax.experimental import pallas as pl
from jax.experimental.pallas import tpu as pltpu
from jax.sharding import PartitionSpec as P

D = 4096
TQ = 112
BLOCK = 64
TP = 192
POOL = 128
NX = 4
NZ = 16
NY = 4
OWNERS = NX * NZ
CAP = 4
CHUNKS = 4
PER = OWNERS // CHUNKS
SLOTS = PER * CAP
W = D // 4
INV_ROOT = 1.0 / math.sqrt(D)
MESH = pl.DeviceIdType.MESH
F32 = jnp.float32
BF16 = jnp.bfloat16


def iota(shape, axis):
    return lax.broadcasted_iota(jnp.int32, shape, axis)


def onehot(mask):
    return jnp.where(mask, 1.0, 0.0).astype(BF16)


def full_kernel(
    q_ref, cl_ref, bl_ref, pos_ref, p_ref, piece_ref, scale_ref,
    home_ref, pg_ref, poolg_ref, loss_ref, sgrad_ref,
    snd, rcv, msnd, mrcv, gsnd, grcv, stack, routed, low, lowt, acc, gp, pool,
    pt, rc, s1, ry, s2, rx, zb, rz, fin, gb, sc, rcs, rys, rxs,
    d_send, d_recv, m_send, m_recv, g_send, g_recv, p_send, p_recv, r_send, r_recv, t_send, t_recv,
):
    grp = lax.axis_index("group")
    clu = lax.axis_index("cluster")
    y, core = grp // 2, grp % 2
    z, x = clu // NX, clu % NX

    def cluster_peer(dz, dx):
        return (grp, ((z + dz + NZ) % NZ) * NX + (x + dx + NX) % NX)

    def group_peer(py, pc):
        return (py * 2 + pc, clu)

    def offset(o):
        return ((o // 4) % 4) * 4 + o // 16, o % 4

    def copy(src, dst, send, recv, peer):
        return pltpu.make_async_remote_copy(
            src_ref=src, dst_ref=dst, send_sem=send, recv_sem=recv, device_id=peer, device_id_type=MESH
        )

    here = (grp, clu)
    barrier = pltpu.get_barrier_semaphore()

    def greet(o, carry):
        dz, dx = offset(o)
        pl.semaphore_signal(barrier, inc=1, device_id=cluster_peer(dz, dx), device_id_type=MESH)
        return carry

    lax.fori_loop(1, OWNERS, greet, 0)

    def greet_group(k, carry):
        pl.semaphore_signal(barrier, inc=1, device_id=((grp + k) % 8, clu), device_id_type=MESH)
        return carry

    lax.fori_loop(1, 8, greet_group, 0)

    factor = scale_ref[0] * INV_ROOT

    a_iota, b_iota = iota((TQ, TQ), 0), iota((TQ, TQ), 1)
    eye = a_iota == b_iota

    def to_col(row):
        return jnp.sum(jnp.where(eye, row.astype(F32), 0.0), axis=1, keepdims=True)

    cl_row = cl_ref[...]
    cl_col = to_col(cl_row).astype(jnp.int32)
    same = cl_col == cl_row
    rank_row = jnp.sum(jnp.where(same & (a_iota < b_iota), 1.0, 0.0), axis=0, keepdims=True).astype(jnp.int32)
    rank_col = jnp.sum(jnp.where(same & (b_iota < a_iota), 1.0, 0.0), axis=1, keepdims=True).astype(jnp.int32)

    def offset_of(cl):
        dz = ((cl >> 2) - z) & 15
        return (dz & 3) * 16 + (dz >> 2) * 4 + ((cl - x) & 3)

    off_row, off_col = offset_of(cl_row), offset_of(cl_col)
    place_row = off_row * 16 + rank_row
    place_col = off_col * 16 + rank_col

    lane = iota((TQ, 128), 1)
    field = lane >> 2
    block0, block1, position = to_col(bl_ref[0:1, :]), to_col(bl_ref[1:2, :]), to_col(pos_ref[...])
    value = jnp.where(field == 0, block0, jnp.where(field == 1, block1, jnp.where(field == 2, position, 1.0)))
    value = jnp.where((rank_col == (lane & 3)) & (field < 4), value, 0.0).astype(BF16)
    meta = jnp.dot(onehot(iota((OWNERS, TQ), 0) == off_row), value, preferred_element_type=F32)
    msnd[:, 0, :] = meta

    def build(c, carry):
        row = iota((PER * 16, TQ), 0) + c * (PER * 16)
        total = jnp.zeros((PER * 16, W), F32)
        for b in range(4):
            pick = onehot(row == place_row + 4 * b)
            total = total + jnp.dot(pick, q_ref[:, b * W:(b + 1) * W], preferred_element_type=F32)
        snd[pl.ds(c * PER, PER)] = total.astype(BF16).reshape(PER, 16, W)
        return carry

    def send_chunk(c):
        def step(o, carry):
            dz, dx = offset(o)
            peer = cluster_peer(dz, dx)
            copy(msnd.at[o], mrcv.at[o], m_send, m_recv.at[o // PER], peer).start()
            copy(snd.at[o], rcv.at[o], d_send, d_recv.at[o // PER], peer).start()
            return carry

        lax.fori_loop(1 if c == 0 else c * PER, (c + 1) * PER, step, 0)

    build(0, 0)
    gp[y, x, z] = piece_ref[y]
    pl.semaphore_wait(barrier, OWNERS - 1 + 7)

    def pool_z(k, carry):
        copy(gp.at[y, x, z], gp.at[y, x, z], p_send.at[0], p_recv.at[0], cluster_peer(k, 0)).start()
        return carry

    lax.fori_loop(1, NZ, pool_z, 0)
    for c in range(CHUNKS):
        send_chunk(c)
        if c + 1 < CHUNKS:
            build(c + 1, 0)
    rcv[0] = snd[0]
    mrcv[0] = msnd[0]

    some = gp.at[y, x, pl.ds(0, NZ - 1)]
    copy(some, some, p_send.at[0], p_recv.at[0], here).wait()
    for k in range(1, NX):
        copy(gp.at[y, x], gp.at[y, x], p_send.at[1], p_recv.at[1], cluster_peer(0, k)).start()
    some = gp.at[y, pl.ds(0, NX - 1)]
    copy(some, some, p_send.at[1], p_recv.at[1], here).wait()
    for k in range(1, NY):
        copy(gp.at[y], gp.at[y], p_send.at[2], p_recv.at[2], group_peer((y + k) % NY, core)).start()
    some = gp.at[pl.ds(0, NY - 1)]
    copy(some, some, p_send.at[2], p_recv.at[2], here).wait()

    def spread(yy, carry):
        flat = gp[yy].reshape(OWNERS * 16, 128)
        i, j = iota((POOL, OWNERS * 16), 0), iota((POOL, OWNERS * 16), 1)
        base = (i >> 5) * (NZ * 16) + (i & 15) * 16 + ((i >> 4) & 1) * 8
        for cb in range(8):
            part = jnp.dot(onehot(j == base + cb), flat, preferred_element_type=F32).astype(BF16)
            pool[:, pl.ds(pl.multiple_of(yy * W + cb * 128, 128), 128)] = part
        return carry

    lax.fori_loop(0, NY, spread, 0)

    i, j = iota((256, 256), 0), iota((256, 256), 1)
    unmix = onehot(((i >> 2) & 15) * 16 + (i >> 6) * 4 + (i & 3) == j)
    mix = onehot(((j >> 2) & 15) * 16 + (j >> 6) * 4 + (j & 3) == i)
    contract = (((1,), (1,)), ((), ()))

    def work(c, carry):
        loss_sum, scale_sum = carry
        some = rcv.at[pl.ds(c * PER, PER)]
        rows = rcv[pl.ds(c * PER, PER)].reshape(PER * 16, W)
        plain = jnp.dot(unmix, rows, preferred_element_type=F32).astype(BF16)
        for b in range(4):
            routed[pl.ds(c * SLOTS, SLOTS), b * W:(b + 1) * W] = plain[b * SLOTS:(b + 1) * SLOTS]
        mine = routed[pl.ds(c * SLOTS, SLOTS), :]
        raw_blk = lax.dot_general(mine, p_ref[...], contract, preferred_element_type=F32)
        raw_pool = lax.dot_general(mine, pool[...], contract, preferred_element_type=F32)
        expand = onehot((iota((SLOTS, PER), 0) >> 2) == iota((SLOTS, PER), 1))
        got = mrcv[pl.ds(c * PER, PER), 0, :].astype(BF16)
        got = jnp.dot(expand, got, preferred_element_type=F32)
        lanes, rank = iota((SLOTS, 128), 1), iota((SLOTS, 128), 0) & 3

        def column(f):
            return jnp.sum(jnp.where(lanes == 4 * f + rank, got, 0.0), axis=1, keepdims=True)

        first, second, place, weight = column(0), column(1), column(2), column(3)
        cand = iota((SLOTS, TP), 1)
        block = (cand >> 6).astype(F32)
        allowed = (block == first) | (block == second)
        hit = cand.astype(F32) == first * BLOCK + place
        score_blk = factor * raw_blk
        score_pool = factor * raw_pool
        peak = jnp.maximum(
            jnp.max(jnp.where(allowed, score_blk, -jnp.inf), axis=1, keepdims=True),
            jnp.max(score_pool, axis=1, keepdims=True),
        )
        exp_blk = jnp.where(allowed, jnp.exp(jnp.where(allowed, score_blk - peak, 0.0)), 0.0)
        exp_pool = jnp.exp(score_pool - peak)
        total = jnp.sum(exp_blk, axis=1, keepdims=True) + jnp.sum(exp_pool, axis=1, keepdims=True)
        log_total = peak + jnp.log(total)
        score_pos = jnp.sum(jnp.where(hit, score_blk, 0.0), axis=1, keepdims=True)
        loss_sum = loss_sum + jnp.sum(weight * (log_total - score_pos), axis=0, keepdims=True)
        grad_blk = weight * (exp_blk / total - jnp.where(hit, 1.0, 0.0))
        grad_pool = weight * (exp_pool / total)
        both = jnp.sum(grad_blk * raw_blk, axis=1, keepdims=True) + jnp.sum(grad_pool * raw_pool, axis=1, keepdims=True)
        scale_sum = scale_sum + INV_ROOT * jnp.sum(both, axis=0, keepdims=True)
        low[pl.ds(c * SLOTS, SLOTS), 0:TP] = grad_blk
        low[pl.ds(c * SLOTS, SLOTS), 256:256 + POOL] = grad_pool
        low_blk, low_pool = grad_blk.astype(BF16), grad_pool.astype(BF16)
        for b in range(4):
            cols = slice(b * W, (b + 1) * W)
            part = jnp.dot(low_blk, p_ref[:, cols], preferred_element_type=F32)
            part = part + jnp.dot(low_pool, pool[:, cols], preferred_element_type=F32)
            stack[b * SLOTS:(b + 1) * SLOTS, :] = (factor * part).astype(BF16)
        mixed = jnp.dot(mix, stack[...], preferred_element_type=F32).astype(BF16)
        gsnd[pl.ds(c * PER, PER)] = mixed.reshape(PER, 16, W)
        return loss_sum, scale_sum

    def bundles(ref, c):
        lo = 1 if c == 0 else c * PER
        return ref.at[pl.ds(lo, (c + 1) * PER - lo)]

    def owner_step(c, sums):
        some = bundles(rcv, c)
        copy(some, some, d_send, d_recv.at[c], here).wait_recv()
        some = bundles(mrcv, c)
        copy(some, some, m_send, m_recv.at[c], here).wait_recv()
        sums = work(c, sums)

        def back(o, carry):
            dz, dx = offset(o)
            copy(gsnd.at[o], grcv.at[o], g_send, g_recv.at[o // PER], cluster_peer(-dz, -dx)).start()
            return carry

        lax.fori_loop(1 if c == 0 else c * PER, (c + 1) * PER, back, 0)
        return sums

    sums = (jnp.zeros((1, 1), F32), jnp.zeros((1, 1), F32))
    for c in range(CHUNKS):
        sums = owner_step(c, sums)
    grcv[0] = gsnd[0]

    low[:, TP:256] = jnp.zeros((256, 256 - TP), F32)
    lowt[...] = low[...].T.astype(BF16)

    def pool_term(k, carry):
        cols = pl.ds(pl.multiple_of(k * 512, 512), 512)
        part = jnp.dot(lowt[256:256 + POOL, :], routed[:, cols], preferred_element_type=F32)
        pt[k % 2, k // 2] = factor * part
        return carry

    lax.fori_loop(0, 8, pool_term, 0)
    tile_lane = iota((8, 128), 1)
    sc[0] = jnp.where(tile_lane == 0, sums[0], jnp.where(tile_lane == 1, sums[1], 0.0))

    peer = group_peer(y, 1 - core)
    move = [
        copy(pt.at[1 - core], rc, r_send.at[0], r_recv.at[0], peer),
        copy(sc.at[0], rcs, t_send.at[0], t_recv.at[0], peer),
    ]
    for one in move:
        one.start()

    def passage_term(k, carry):
        cols = pl.ds(pl.multiple_of(k * 512, 512), 512)
        part = jnp.dot(lowt[0:TP, :], routed[:, cols], preferred_element_type=F32)
        pg_ref[:, cols] = (factor * part).astype(BF16)
        return carry

    lax.fori_loop(0, 8, passage_term, 0)
    for one in move:
        one.wait()
    s1[...] = pt[core] + rc[...]
    sc[1] = sc[0] + rcs[...]

    for k in range(1, NY):
        to = (y + k) % NY
        copy(s1.at[to], ry.at[k - 1], r_send.at[1], r_recv.at[1], group_peer(to, core)).start()
        copy(sc.at[1], rys.at[k - 1], t_send.at[1], t_recv.at[1], group_peer(to, core)).start()
    copy(ry, ry, r_send.at[1], r_recv.at[1], here).wait()
    copy(rys, rys, t_send.at[1], t_recv.at[1], here).wait()
    s2[...] = (s1[y] + ry[0] + ry[1] + ry[2]).reshape(NX, 32, 512)
    sc[2] = sc[1] + rys[0] + rys[1] + rys[2]

    for k in range(1, NX):
        to = (x + k) % NX
        copy(s2.at[to], rx.at[k - 1], r_send.at[2], r_recv.at[2], cluster_peer(0, k)).start()
        copy(sc.at[2], rxs.at[k - 1], t_send.at[2], t_recv.at[2], cluster_peer(0, k)).start()
    copy(rx, rx, r_send.at[2], r_recv.at[2], here).wait()
    copy(rxs, rxs, t_send.at[2], t_recv.at[2], here).wait()
    s3 = s2[x] + rx[0] + rx[1] + rx[2]
    scalars = sc[2] + rxs[0] + rxs[1] + rxs[2]
    for r in range(2):
        for cb in range(4):
            zb[:, r * 4 + cb, :] = s3[r * NZ:(r + 1) * NZ, cb * 128:(cb + 1) * 128]
    zb[:, 8:16, :] = jnp.broadcast_to(scalars[None], (NZ, 8, 128))

    def to_z(k, carry):
        copy(zb.at[(z + k) % NZ], rz.at[k - 1], r_send.at[3], r_recv.at[3], cluster_peer(k, 0)).start()
        return carry

    lax.fori_loop(1, NZ, to_z, 0)
    copy(rz, rz, r_send.at[3], r_recv.at[3], here).wait()
    last = zb[z] + jnp.sum(rz[...], axis=0)
    fin[...] = last[0:8]
    gb[grp] = last[0:8]
    loss_ref[0] = jnp.sum(jnp.where(tile_lane[0:1] == 0, last[8:9], 0.0)) * (1.0 / (TQ * OWNERS * 8))
    sgrad_ref[0] = jnp.sum(jnp.where(tile_lane[0:1] == 1, last[8:9], 0.0))

    def to_group(k, carry):
        copy(fin, gb.at[grp], r_send.at[4], r_recv.at[4], ((grp + k) % 8, clu)).start()
        return carry

    lax.fori_loop(1, 8, to_group, 0)

    def take(c):
        some = bundles(grcv, c)
        copy(some, some, g_send, g_recv.at[c], here).wait_recv()
        rows = grcv[pl.ds(c * PER, PER)].reshape(PER * 16, W)
        lanes = iota((TQ, PER * 16), 1) + c * (PER * 16)
        for b in range(4):
            part = jnp.dot(onehot(lanes == place_col + 4 * b), rows, preferred_element_type=F32)
            if c == 0:
                acc[:, b * W:(b + 1) * W] = part
            elif c + 1 < CHUNKS:
                acc[:, b * W:(b + 1) * W] += part
            else:
                home_ref[:, b * W:(b + 1) * W] = (acc[:, b * W:(b + 1) * W] + part).astype(BF16)

    for c in range(CHUNKS):
        take(c)

    some = gb.at[pl.ds(0, 7)]
    copy(some, some, r_send.at[4], r_recv.at[4], here).wait()
    for g in range(8):
        for r in range(2):
            for cb in range(4):
                col = g * 512 + cb * 128
                poolg_ref[r:r + 1, col:col + 128] = gb[g, r * 4 + cb:r * 4 + cb + 1, :]

    some = rcv.at[pl.ds(1, OWNERS - 1)]
    copy(some, some, d_send, d_recv.at[0], here).wait_send()
    copy(some, some, g_send, g_recv.at[0], here).wait_send()
    some = mrcv.at[pl.ds(1, OWNERS - 1)]
    copy(some, some, m_send, m_recv.at[0], here).wait_send()


BASE = 2
V = D // 8
SPARE = 12
RING = 4 * SPARE
LATE = 2 * NZ


def fast_kernel(
    q_ref, cl_ref, bl_ref, pos_ref, p_ref, piece_ref, scale_ref,
    home_ref, pg_ref, poolg_ref, loss_ref, sgrad_ref, flag_ref,
    snd, rcv, msnd, mrcv, gsnd, grcv, stack, routed, low, lowt, acc, gp, pool,
    og, tg, px, pv, pts, ptr, rsn, rv, cc, rr, ll, late,
    pt, rc, s1, ry, s2, rx, zb, rz, fin, gb, sc, rcs, rys, rxs,
    d_send, d_recv, m_send, m_recv, g_send, g_recv, p_send, p_recv, r_send, r_recv, t_send, t_recv,
    f_send, fr_recv, fl_recv, b_send, br_recv, bl_recv, x_send, x_recv,
):
    grp = lax.axis_index("group")
    clu = lax.axis_index("cluster")
    y, core = grp // 2, grp % 2
    z, x = clu // NX, clu % NX

    def cluster_peer(dz, dx):
        return (grp, ((z + dz + NZ) % NZ) * NX + (x + dx + NX) % NX)

    def group_peer(py, pc):
        return (py * 2 + pc, clu)

    def offset(o):
        return ((o // 4) % 4) * 4 + o // 16, o % 4

    def copy(src, dst, send, recv, peer):
        return pltpu.make_async_remote_copy(
            src_ref=src, dst_ref=dst, send_sem=send, recv_sem=recv, device_id=peer, device_id_type=MESH
        )

    here = (grp, clu)
    barrier = pltpu.get_barrier_semaphore()

    def greet(o, carry):
        dz, dx = offset(o)
        pl.semaphore_signal(barrier, inc=1, device_id=cluster_peer(dz, dx), device_id_type=MESH)
        return carry

    lax.fori_loop(1, OWNERS, greet, 0)

    def greet_group(k, carry):
        pl.semaphore_signal(barrier, inc=1, device_id=((grp + k) % 8, clu), device_id_type=MESH)
        return carry

    lax.fori_loop(1, 8, greet_group, 0)

    factor = scale_ref[0] * INV_ROOT

    a_iota, b_iota = iota((TQ, TQ), 0), iota((TQ, TQ), 1)
    eye = a_iota == b_iota

    def to_col(row):
        return jnp.sum(jnp.where(eye, row.astype(F32), 0.0), axis=1, keepdims=True)

    cl_row = cl_ref[...]
    cl_col = to_col(cl_row).astype(jnp.int32)
    same = cl_col == cl_row
    rank_row = jnp.sum(jnp.where(same & (a_iota < b_iota), 1.0, 0.0), axis=0, keepdims=True).astype(jnp.int32)
    rank_col = jnp.sum(jnp.where(same & (b_iota < a_iota), 1.0, 0.0), axis=1, keepdims=True).astype(jnp.int32)
    extra_row, extra_col = rank_row >= BASE, rank_col >= BASE
    spare_row = jnp.sum(jnp.where(extra_col & (a_iota < b_iota), 1.0, 0.0), axis=0, keepdims=True).astype(jnp.int32)
    spare_col = jnp.sum(jnp.where(extra_row & (b_iota < a_iota), 1.0, 0.0), axis=1, keepdims=True).astype(jnp.int32)
    fits_row, fits_col = extra_row & (spare_row < SPARE), extra_col & (spare_col < SPARE)
    spare_row = jnp.where(fits_row, spare_row, -4096)
    spare_col = jnp.where(fits_col, spare_col, -4096)
    left_over = jnp.sum(jnp.where(extra_col & jnp.logical_not(fits_col), 1.0, 0.0), axis=0, keepdims=True)

    def offset_of(cl):
        dz = ((cl >> 2) - z) & 15
        return (dz & 3) * 16 + (dz >> 2) * 4 + ((cl - x) & 3)

    off_row, off_col = offset_of(cl_row), offset_of(cl_col)
    place_row = jnp.where(extra_row, -4096, off_row * 16 + rank_row)
    place_col = jnp.where(extra_col, -4096, off_col * 16 + rank_col)

    lane = iota((TQ, 128), 1)
    field = lane >> 2
    block0, block1, position = to_col(bl_ref[0:1, :]), to_col(bl_ref[1:2, :]), to_col(pos_ref[...])
    value = jnp.where(field == 0, block0, jnp.where(field == 1, block1, jnp.where(field == 2, position, 1.0)))
    value = jnp.where((rank_col == (lane & 3)) & (field < 4) & jnp.logical_not(extra_col), value, 0.0).astype(BF16)
    meta = jnp.dot(onehot(iota((OWNERS, TQ), 0) == off_row), value, preferred_element_type=F32)
    msnd[:, 0, :] = meta

    def spot_of(d):
        return (d + 3) % NZ

    total = jnp.zeros((RING, W), F32)
    for b in range(4):
        pick = onehot(iota((RING, TQ), 0) == spare_row + SPARE * b)
        total = total + jnp.dot(pick, q_ref[:, b * W:(b + 1) * W], preferred_element_type=F32)
    og[spot_of(0)] = total.astype(BF16)
    kind = iota((8, TQ), 0)
    facts = jnp.where(
        kind == 0, cl_row.astype(F32),
        jnp.where(
            kind == 1, bl_ref[0:1, :].astype(F32),
            jnp.where(kind == 2, bl_ref[1:2, :].astype(F32), jnp.where(kind == 3, pos_ref[...].astype(F32), 1.0)),
        ),
    )
    facts = jnp.where(kind < 5, facts, 0.0).astype(BF16)
    spot = lane % SPARE
    tg[spot_of(0)] = jnp.dot(facts, onehot((spot == spare_col) & (lane < RING)), preferred_element_type=F32)

    def build(c):
        row = iota((PER * 16, TQ), 0) + c * (PER * 16)
        total = jnp.zeros((PER * 16, V), F32)
        for b in range(8):
            pick = onehot(row == place_row + BASE * b)
            total = total + jnp.dot(pick, q_ref[:, b * V:(b + 1) * V], preferred_element_type=F32)
        snd[pl.ds(c * PER, PER)] = total.astype(BF16).reshape(PER, 16, V)

    EIGHT = OWNERS // 8

    def send(e):
        def step(o, carry):
            dz, dx = offset(o)
            peer = cluster_peer(dz, dx)
            copy(msnd.at[o], mrcv.at[o], m_send, m_recv.at[o // PER], peer).start()
            copy(snd.at[o], rcv.at[o], d_send, d_recv.at[o // PER], peer).start()
            return carry

        lax.fori_loop(1 if e == 0 else e * EIGHT, (e + 1) * EIGHT, step, 0)

    def ring(k):
        if k > 1:
            if k <= 8:
                one = og.at[0]
                copy(one, one, f_send.at[0], fr_recv.at[k - 2], here).wait_recv()
            one = og.at[0]
            copy(one, one, f_send.at[1], fl_recv.at[k - 2], here).wait_recv()
        if k < 8:
            copy(
                og.at[spot_of(1 - k)], og.at[spot_of(-k)], f_send.at[0], fr_recv.at[k - 1], cluster_peer(1, 0)
            ).start()
        copy(og.at[spot_of(k - 1)], og.at[spot_of(k)], f_send.at[1], fl_recv.at[k - 1], cluster_peer(-1, 0)).start()

    def spread():
        i, j = iota((8 * POOL, OWNERS * 16), 0), iota((8 * POOL, OWNERS * 16), 1)
        at = i & 127
        order = onehot(j == (at >> 5) * (NZ * 16) + (at & 15) * 16 + ((at >> 4) & 1) * 8 + (i >> 7))
        for pair in range(2):
            flat = jnp.concatenate(
                [gp[2 * pair].reshape(OWNERS * 16, 128), gp[2 * pair + 1].reshape(OWNERS * 16, 128)], axis=1
            )
            part = jnp.dot(order, flat, preferred_element_type=F32).astype(BF16)
            for cb in range(8):
                for one in range(2):
                    col = (2 * pair + one) * W + cb * 128
                    pool[:, col:col + 128] = part[cb * 128:(cb + 1) * 128, one * 128:(one + 1) * 128]

    def gather_facts(k, carry):
        source = iota((128, NZ * RING), 0)
        shift = onehot((iota((128, NZ * RING), 1) == source + k * RING) & (source < RING))
        return carry + jnp.dot(tg[k].astype(BF16), shift, preferred_element_type=F32)

    gp[y, x, z] = piece_ref[y]
    build(0)
    build(1)
    pl.semaphore_wait(barrier, OWNERS - 1 + 7)
    ring(1)

    def early(k, carry):
        copy(tg.at[spot_of(0)], tg.at[(19 - k) % NZ], t_send.at[3], t_recv.at[3], cluster_peer(k, 0)).start()
        copy(gp.at[y, x, z], gp.at[y, x, z], p_send.at[0], p_recv.at[0], cluster_peer(k, 0)).start()
        return carry

    lax.fori_loop(1, NZ, early, 0)
    send(0)
    ring(2)
    send(1)
    build(2)
    ring(3)
    send(2)
    some = gp.at[y, x, pl.ds(0, NZ - 1)]
    copy(some, some, p_send.at[0], p_recv.at[0], here).wait()
    for k in range(1, NX):
        copy(gp.at[y, x], gp.at[y, x], p_send.at[1], p_recv.at[1], cluster_peer(0, k)).start()
    build(3)
    ring(4)
    send(3)

    some = tg.at[pl.ds(0, NZ - 1)]
    copy(some, some, t_send.at[3], t_recv.at[3], here).wait()
    span = NZ * RING
    known = lax.fori_loop(0, NZ // 2, gather_facts, jnp.zeros((8, span), F32))
    ring(5)
    send(4)
    known = lax.fori_loop(NZ // 2, NZ, gather_facts, known)
    some = gp.at[y, pl.ds(0, NX - 1)]
    copy(some, some, p_send.at[1], p_recv.at[1], here).wait()
    for k in range(1, NY):
        copy(gp.at[y], gp.at[y], p_send.at[2], p_recv.at[2], group_peer((y + k) % NY, core)).start()
    ring(6)
    dest = known[0:1].astype(jnp.int32)
    local = (known[4:5] > 0.5) & ((dest >> 2) == z)
    across = iota((1, span), 1)
    block_of = (across % RING) // SPARE
    part_of = jnp.where(across >= span // 2, 1, 0)
    to_x = dest & 3
    mark = (iota((8, span), 0) == part_of * NX + to_x) & local & (block_of == 0)
    before = onehot(iota((span, span), 0) < across - block_of * SPARE)
    ranks = jnp.dot(onehot(mark), before, preferred_element_type=F32)
    order = jnp.sum(jnp.where(iota((8, span), 0) == part_of * NX + to_x, ranks, 0.0), axis=0, keepdims=True).astype(jnp.int32)
    key = jnp.where(local, to_x * (4 * NZ) + block_of * NZ + order, -1)
    first_key = jnp.where(local & (block_of == 0), to_x * LATE + part_of * NZ + order, -1)
    key_col = jnp.broadcast_to(key.astype(F32), (8, span)).T[:, 0:1].astype(jnp.int32)
    pts[...] = lax.dot_general(
        known.astype(BF16), onehot(iota((NX * LATE, span), 0) == first_key), (((1,), (1,)), ((), ())),
        preferred_element_type=F32,
    )

    MIX = NX * 4 * NZ
    HS = span // 2

    def hand_on(h):
        pick = onehot(iota((MIX, HS), 0) == key[:, h * HS:(h + 1) * HS])
        for ct in range(2):
            cols = slice(ct * 512, (ct + 1) * 512)
            held = og[h * 8:(h + 1) * 8, :, cols].reshape(HS, 512)
            part = jnp.dot(pick, held, preferred_element_type=F32).astype(BF16)
            px[h, :, :, cols] = part.reshape(NX, 4 * NZ, 512)
        for k in range(1, NX):
            copy(px.at[h, (x + k) % NX], pv.at[h, x], x_send.at[h], x_recv.at[h], cluster_peer(0, k)).start()
        pv[h, x] = px[h, x]

    hand_on(0)
    for k in range(1, NX):
        copy(pts, ptr.at[x], x_send.at[2], x_recv.at[2], cluster_peer(0, k)).start()
    ptr[x] = pts[...]
    ring(7)
    rcv[0] = snd[0]
    mrcv[0] = msnd[0]
    ring(8)
    send(5)
    one = og.at[0]
    copy(one, one, f_send.at[1], fl_recv.at[7], here).wait_recv()
    hand_on(1)
    send(6)
    send(7)
    some = gp.at[pl.ds(0, NY - 1)]
    copy(some, some, p_send.at[2], p_recv.at[2], here).wait()
    spread()

    i, j = iota((256, 256), 0), iota((256, 256), 1)
    unmix = onehot(((i >> 1) & 15) * 16 + (i >> 5) * 2 + (i & 1) == j)
    mix = onehot(((j >> 1) & 15) * 16 + (j >> 5) * 2 + (j & 1) == i)
    contract = (((1,), (1,)), ((), ()))

    def work(lo, count, columns, sums):
        loss_sum, scale_sum = sums
        first, second, place, weight = columns
        mine = routed[lo:lo + count, :]
        raw_blk = lax.dot_general(mine, p_ref[...], contract, preferred_element_type=F32)
        raw_pool = lax.dot_general(mine, pool[...], contract, preferred_element_type=F32)
        cand = iota((count, TP), 1)
        block = (cand >> 6).astype(F32)
        allowed = (block == first) | (block == second)
        hit = cand.astype(F32) == first * BLOCK + place
        score_blk = factor * raw_blk
        score_pool = factor * raw_pool
        peak = jnp.maximum(
            jnp.max(jnp.where(allowed, score_blk, -jnp.inf), axis=1, keepdims=True),
            jnp.max(score_pool, axis=1, keepdims=True),
        )
        exp_blk = jnp.where(allowed, jnp.exp(jnp.where(allowed, score_blk - peak, 0.0)), 0.0)
        exp_pool = jnp.exp(score_pool - peak)
        total = jnp.sum(exp_blk, axis=1, keepdims=True) + jnp.sum(exp_pool, axis=1, keepdims=True)
        log_total = peak + jnp.log(total)
        score_pos = jnp.sum(jnp.where(hit, score_blk, 0.0), axis=1, keepdims=True)
        loss_sum = loss_sum + jnp.sum(weight * (log_total - score_pos), axis=0, keepdims=True)
        grad_blk = weight * (exp_blk / total - jnp.where(hit, 1.0, 0.0))
        grad_pool = weight * (exp_pool / total)
        both = jnp.sum(grad_blk * raw_blk, axis=1, keepdims=True) + jnp.sum(grad_pool * raw_pool, axis=1, keepdims=True)
        scale_sum = scale_sum + INV_ROOT * jnp.sum(both, axis=0, keepdims=True)
        low[lo:lo + count, 0:TP] = grad_blk
        low[lo:lo + count, 256:256 + POOL] = grad_pool
        low_blk, low_pool = grad_blk.astype(BF16), grad_pool.astype(BF16)

        def grads(cols):
            part = jnp.dot(low_blk, p_ref[:, cols], preferred_element_type=F32)
            part = part + jnp.dot(low_pool, pool[:, cols], preferred_element_type=F32)
            return (factor * part).astype(BF16)

        return (loss_sum, scale_sum), grads

    def bundles(ref, c):
        lo = 1 if c == 0 else c * PER
        return ref.at[pl.ds(lo, (c + 1) * PER - lo)]

    HALF = 2 * PER * BASE

    def half(h, sums):
        for c in (2 * h, 2 * h + 1):
            some = bundles(rcv, c)
            copy(some, some, d_send, d_recv.at[c], here).wait_recv()
            some = bundles(mrcv, c)
            copy(some, some, m_send, m_recv.at[c], here).wait_recv()
            rows = rcv[pl.ds(c * PER, PER)].reshape(PER * 16, V)
            plain = jnp.dot(unmix, rows, preferred_element_type=F32).astype(BF16)
            for b in range(8):
                routed[c * 32:(c + 1) * 32, b * V:(b + 1) * V] = plain[b * 32:(b + 1) * 32]
        expand = onehot((iota((HALF, 2 * PER), 0) >> 1) == iota((HALF, 2 * PER), 1))
        got = mrcv[pl.ds(2 * h * PER, 2 * PER), 0, :].astype(BF16)
        got = jnp.dot(expand, got, preferred_element_type=F32)
        lanes, rank = iota((HALF, 128), 1), iota((HALF, 128), 0) & 1

        def column(f):
            return jnp.sum(jnp.where(lanes == 4 * f + rank, got, 0.0), axis=1, keepdims=True)

        sums, grads = work(h * HALF, HALF, [column(f) for f in range(4)], sums)
        for b in range(8):
            part = grads(slice(b * V, (b + 1) * V))
            stack[0, b * 32:(b + 1) * 32, :] = part[0:32]
            stack[1, b * 32:(b + 1) * 32, :] = part[32:64]
        for c in (0, 1):
            mixed = jnp.dot(mix, stack[c], preferred_element_type=F32).astype(BF16)
            gsnd[pl.ds((2 * h + c) * PER, PER)] = mixed.reshape(PER, 16, V)
        return sums

    def send_back(e):
        def back(o, carry):
            dz, dx = offset(o)
            copy(gsnd.at[o], grcv.at[o], g_send, g_recv.at[o // PER], cluster_peer(-dz, -dx)).start()
            return carry

        lax.fori_loop(1 if e == 0 else e * EIGHT, (e + 1) * EIGHT, back, 0)

    sums = (jnp.zeros((1, 1), F32), jnp.zeros((1, 1), F32))
    sums = half(0, sums)
    for e in range(4):
        send_back(e)
    grcv[0] = gsnd[0]

    for h in range(2):
        some = pv.at[h, pl.ds(0, NX - 1)]
        copy(some, some, x_send.at[h], x_recv.at[h], here).wait()
    some = ptr.at[pl.ds(0, NX - 1)]
    copy(some, some, x_send.at[2], x_recv.at[2], here).wait()
    choose = onehot(iota((LATE, 128), 1) == iota((LATE, 128), 0) + x * LATE)
    for via in range(NX):
        for h in range(2):
            lo = 128 + via * LATE + h * NZ
            for b in range(4):
                routed[lo:lo + NZ, b * W:(b + 1) * W] = pv[h, via, b * NZ:(b + 1) * NZ, :]
        late[via * LATE:(via + 1) * LATE, 0:8] = lax.dot_general(
            choose, ptr[via].astype(BF16), contract, preferred_element_type=F32
        )
    sums, grads = work(128, 128, [late[:, f:f + 1] for f in range(1, 5)], sums)
    for b in range(4):
        part = grads(slice(b * W, (b + 1) * W))
        for via in range(NX):
            for h in range(2):
                lo = via * LATE + h * NZ
                rsn[h, via, b * NZ:(b + 1) * NZ, :] = part[lo:lo + NZ]
    for h in (1, 0):
        for k in range(1, NX):
            copy(rsn.at[h, (x + k) % NX], rv.at[h, x], x_send.at[3 + h], x_recv.at[3 + h], cluster_peer(0, k)).start()
        rv[h, x] = rsn[h, x]

    def share(h):
        some = rv.at[h, pl.ds(0, NX - 1)]
        copy(some, some, x_send.at[3 + h], x_recv.at[3 + h], here).wait()
        pick = onehot(iota((HS, MIX), 1) == key_col[h * HS:(h + 1) * HS])
        for ct in range(2):
            cols = slice(ct * 512, (ct + 1) * 512)
            back = rv[h, :, :, cols].reshape(MIX, 512)
            part = jnp.dot(pick, back, preferred_element_type=F32).astype(BF16)
            cc[h * 8:(h + 1) * 8, :, cols] = part.reshape(8, RING, 512)

    share(1)

    def ring_back(k):
        to = spot_of(9 - k)
        if k > 1:
            copy(rr.at[k - 2], rr.at[k - 2], b_send.at[0], br_recv.at[k - 2], here).wait_recv()
            cc[to] = cc[to] + rr[k - 2]
        copy(cc.at[to], rr.at[k - 1], b_send.at[0], br_recv.at[k - 1], cluster_peer(1, 0)).start()
        if k < 8:
            to = spot_of(k - 8)
            if k > 1:
                copy(ll.at[k - 2], ll.at[k - 2], b_send.at[1], bl_recv.at[k - 2], here).wait_recv()
                cc[to] = cc[to] + ll[k - 2]
            copy(cc.at[to], ll.at[k - 1], b_send.at[1], bl_recv.at[k - 1], cluster_peer(-1, 0)).start()

    ring_back(1)
    ring_back(2)
    sums = half(1, sums)
    send_back(4)

    low[:, TP:256] = jnp.zeros((256, 256 - TP), F32)
    lowt[...] = low[...].T.astype(BF16)

    def pool_term(k, carry):
        cols = pl.ds(pl.multiple_of(k * 512, 512), 512)
        part = jnp.dot(lowt[256:256 + POOL, :], routed[:, cols], preferred_element_type=F32)
        pt[k % 2, k // 2] = factor * part
        return carry

    lax.fori_loop(0, 8, pool_term, 0)
    tile_lane = iota((8, 128), 1)
    sc[0] = jnp.where(
        tile_lane == 0, sums[0], jnp.where(tile_lane == 1, sums[1], jnp.where(tile_lane == 2, left_over, 0.0))
    )

    peer = group_peer(y, 1 - core)
    move = [
        copy(pt.at[1 - core], rc, r_send.at[0], r_recv.at[0], peer),
        copy(sc.at[0], rcs, t_send.at[0], t_recv.at[0], peer),
    ]
    for one in move:
        one.start()
    ring_back(3)
    send_back(5)
    share(0)

    def passage_term(k, carry):
        cols = pl.ds(pl.multiple_of(k * 512, 512), 512)
        part = jnp.dot(lowt[0:TP, :], routed[:, cols], preferred_element_type=F32)
        pg_ref[:, cols] = (factor * part).astype(BF16)
        return carry

    lax.fori_loop(0, 4, passage_term, 0)
    ring_back(4)
    send_back(6)
    lax.fori_loop(4, 8, passage_term, 0)
    for one in move:
        one.wait()
    s1[...] = pt[core] + rc[...]
    sc[1] = sc[0] + rcs[...]

    for k in range(1, NY):
        to = (y + k) % NY
        copy(s1.at[to], ry.at[k - 1], r_send.at[1], r_recv.at[1], group_peer(to, core)).start()
        copy(sc.at[1], rys.at[k - 1], t_send.at[1], t_recv.at[1], group_peer(to, core)).start()
    ring_back(5)
    send_back(7)
    copy(ry, ry, r_send.at[1], r_recv.at[1], here).wait()
    copy(rys, rys, t_send.at[1], t_recv.at[1], here).wait()
    s2[...] = (s1[y] + ry[0] + ry[1] + ry[2]).reshape(NX, 32, 512)
    sc[2] = sc[1] + rys[0] + rys[1] + rys[2]

    for k in range(1, NX):
        to = (x + k) % NX
        copy(s2.at[to], rx.at[k - 1], r_send.at[2], r_recv.at[2], cluster_peer(0, k)).start()
        copy(sc.at[2], rxs.at[k - 1], t_send.at[2], t_recv.at[2], cluster_peer(0, k)).start()
    ring_back(6)
    copy(rx, rx, r_send.at[2], r_recv.at[2], here).wait()
    copy(rxs, rxs, t_send.at[2], t_recv.at[2], here).wait()
    s3 = s2[x] + rx[0] + rx[1] + rx[2]
    scalars = sc[2] + rxs[0] + rxs[1] + rxs[2]
    for r in range(2):
        for cb in range(4):
            zb[:, r * 4 + cb, :] = s3[r * NZ:(r + 1) * NZ, cb * 128:(cb + 1) * 128]
    zb[:, 8:16, :] = jnp.broadcast_to(scalars[None], (NZ, 8, 128))

    def to_z(k, carry):
        copy(zb.at[(z + k) % NZ], rz.at[k - 1], r_send.at[3], r_recv.at[3], cluster_peer(k, 0)).start()
        return carry

    lax.fori_loop(1, NZ, to_z, 0)
    ring_back(7)
    copy(rz, rz, r_send.at[3], r_recv.at[3], here).wait()
    last = zb[z] + jnp.sum(rz[...], axis=0)
    fin[...] = last[0:8]
    gb[grp] = last[0:8]
    loss_ref[0] = jnp.sum(jnp.where(tile_lane[0:1] == 0, last[8:9], 0.0)) * (1.0 / (TQ * OWNERS * 8))
    sgrad_ref[0] = jnp.sum(jnp.where(tile_lane[0:1] == 1, last[8:9], 0.0))
    flag_ref[0] = jnp.sum(jnp.where(tile_lane[0:1] == 2, last[8:9], 0.0))

    def to_group(k, carry):
        copy(fin, gb.at[grp], r_send.at[4], r_recv.at[4], ((grp + k) % 8, clu)).start()
        return carry

    lax.fori_loop(1, 8, to_group, 0)
    ring_back(8)

    def take(c):
        some = bundles(grcv, c)
        copy(some, some, g_send, g_recv.at[c], here).wait_recv()
        rows = grcv[pl.ds(c * PER, PER)].reshape(PER * 16, V)
        lanes = iota((TQ, PER * 16), 1) + c * (PER * 16)
        pick = jnp.concatenate([onehot(lanes == place_col + BASE * b) for b in range(8)], axis=0)
        part = jnp.dot(pick, rows, preferred_element_type=F32)
        for b in range(8):
            if c == 0:
                acc[:, b * V:(b + 1) * V] = part[b * TQ:(b + 1) * TQ]
            else:
                acc[:, b * V:(b + 1) * V] += part[b * TQ:(b + 1) * TQ]

    for c in range(CHUNKS):
        take(c)
    copy(rr.at[7], rr.at[7], b_send.at[0], br_recv.at[7], here).wait_recv()
    copy(ll.at[6], ll.at[6], b_send.at[1], bl_recv.at[6], here).wait_recv()
    spare_rows = cc[spot_of(0)] + rr[7] + ll[6]
    for b in range(4):
        pick = onehot(iota((TQ, RING), 1) == spare_col + SPARE * b)
        part = jnp.dot(pick, spare_rows, preferred_element_type=F32)
        home_ref[:, b * W:(b + 1) * W] = (acc[:, b * W:(b + 1) * W] + part).astype(BF16)

    some = gb.at[pl.ds(0, 7)]
    copy(some, some, r_send.at[4], r_recv.at[4], here).wait()
    for g in range(8):
        for r in range(2):
            for cb in range(4):
                col = g * 512 + cb * 128
                poolg_ref[r:r + 1, col:col + 128] = gb[g, r * 4 + cb:r * 4 + cb + 1, :]

    some = rcv.at[pl.ds(1, OWNERS - 1)]
    copy(some, some, d_send, d_recv.at[0], here).wait_send()
    copy(some, some, g_send, g_recv.at[0], here).wait_send()
    some = mrcv.at[pl.ds(1, OWNERS - 1)]
    copy(some, some, m_send, m_recv.at[0], here).wait_send()
    for side, count in ((0, 8), (1, 7)):
        some = og.at[pl.ds(0, 15 - count)]
        copy(some, some, f_send.at[side], fr_recv.at[0], here).wait_send()
        some = cc.at[pl.ds(0, count)]
        copy(some, some, b_send.at[side], br_recv.at[0], here).wait_send()


def reduce_scratch():
    return [
        pltpu.VMEM((2, NY, POOL, 512), F32),
        pltpu.VMEM((NY, POOL, 512), F32),
        pltpu.VMEM((NY, POOL, 512), F32),
        pltpu.VMEM((NY - 1, POOL, 512), F32),
        pltpu.VMEM((NX, 32, 512), F32),
        pltpu.VMEM((NX - 1, 32, 512), F32),
        pltpu.VMEM((NZ, 16, 128), F32),
        pltpu.VMEM((NZ - 1, 16, 128), F32),
        pltpu.VMEM((8, 128), F32),
        pltpu.VMEM((8, 8, 128), F32),
        pltpu.VMEM((3, 8, 128), F32),
        pltpu.VMEM((8, 128), F32),
        pltpu.VMEM((NY - 1, 8, 128), F32),
        pltpu.VMEM((NX - 1, 8, 128), F32),
    ]


def fast_call(*args):
    vm = pl.BlockSpec(memory_space=pltpu.VMEM)
    sm = pl.BlockSpec(memory_space=pltpu.SMEM)
    bundle = pltpu.VMEM((OWNERS, 16, V), BF16)
    note = pltpu.VMEM((OWNERS, 1, 128), F32)
    column = pltpu.VMEM((2, NX, 4 * NZ, W), BF16)
    dma = pltpu.SemaphoreType.DMA
    scalar = jax.ShapeDtypeStruct((1,), F32)
    return pl.pallas_call(
        fast_kernel,
        out_shape=(
            jax.ShapeDtypeStruct((TQ, D), BF16),
            jax.ShapeDtypeStruct((TP, D), BF16),
            jax.ShapeDtypeStruct((2, D), F32),
            scalar, scalar, scalar,
        ),
        in_specs=[vm] * 6 + [sm],
        out_specs=(vm, vm, vm, sm, sm, sm),
        scratch_shapes=[
            bundle, bundle, note, note, bundle, bundle,
            pltpu.VMEM((2, 256, V), BF16),
            pltpu.VMEM((256, D), BF16),
            pltpu.VMEM((256, 384), F32),
            pltpu.VMEM((384, 256), BF16),
            pltpu.VMEM((TQ, D), F32),
            pltpu.VMEM((NY, NX, NZ, 16, 128), BF16),
            pltpu.VMEM((POOL, D), BF16),
            pltpu.VMEM((NZ, RING, W), BF16),
            pltpu.VMEM((NZ, 8, 128), F32),
            column, column,
            pltpu.VMEM((8, 128), F32),
            pltpu.VMEM((NX, 8, 128), F32),
            column, column,
            pltpu.VMEM((NZ, RING, W), BF16),
            pltpu.VMEM((8, RING, W), BF16),
            pltpu.VMEM((7, RING, W), BF16),
            pltpu.VMEM((128, 128), F32),
            *reduce_scratch(),
            dma, dma((CHUNKS,)), dma, dma((CHUNKS,)), dma, dma((CHUNKS,)),
            dma((3,)), dma((3,)), dma((5,)), dma((5,)), dma((4,)), dma((4,)),
            dma((2,)), dma((7,)), dma((8,)), dma((2,)), dma((8,)), dma((7,)), dma((5,)), dma((5,)),
        ],
        compiler_params=pltpu.CompilerParams(
            collective_id=1, has_side_effects=True, vmem_limit_bytes=48 * 1024 * 1024
        ),
        cost_estimate=pl.CostEstimate(flops=4 * 10**9, bytes_accessed=6 * 10**6, transcendentals=82000),
    )(*args)


def full_call(*args):
    vm = pl.BlockSpec(memory_space=pltpu.VMEM)
    sm = pl.BlockSpec(memory_space=pltpu.SMEM)
    bundle = pltpu.VMEM((OWNERS, 16, W), BF16)
    note = pltpu.VMEM((OWNERS, 1, 128), F32)
    dma = pltpu.SemaphoreType.DMA
    return pl.pallas_call(
        full_kernel,
        out_shape=(
            jax.ShapeDtypeStruct((TQ, D), BF16),
            jax.ShapeDtypeStruct((TP, D), BF16),
            jax.ShapeDtypeStruct((2, D), F32),
            jax.ShapeDtypeStruct((1,), F32),
            jax.ShapeDtypeStruct((1,), F32),
        ),
        in_specs=[vm] * 6 + [sm],
        out_specs=(vm, vm, vm, sm, sm),
        scratch_shapes=[
            bundle, bundle, note, note, bundle, bundle,
            pltpu.VMEM((256, W), BF16),
            pltpu.VMEM((256, D), BF16),
            pltpu.VMEM((256, 384), F32),
            pltpu.VMEM((384, 256), BF16),
            pltpu.VMEM((TQ, D), F32),
            pltpu.VMEM((NY, NX, NZ, 16, 128), BF16),
            pltpu.VMEM((POOL, D), BF16),
            *reduce_scratch(),
            dma, dma((CHUNKS,)), dma, dma((CHUNKS,)), dma, dma((CHUNKS,)),
            dma((3,)), dma((3,)), dma((5,)), dma((5,)), dma((3,)), dma((3,)),
        ],
        compiler_params=pltpu.CompilerParams(
            collective_id=0, has_side_effects=True, vmem_limit_bytes=48 * 1024 * 1024
        ),
        cost_estimate=pl.CostEstimate(flops=4 * 10**9, bytes_accessed=6 * 10**6, transcendentals=82000),
    )(*args)


def per_device(queries, cluster_id, block_list, positive, passages, pool_rows, logit_scale):
    piece = pool_rows.reshape(2, 4, 8, 128).transpose(1, 0, 2, 3).reshape(4, 16, 128)
    args = (
        queries,
        cluster_id.reshape(1, TQ),
        block_list.T,
        positive.reshape(1, TQ),
        passages,
        piece,
        logit_scale,
    )
    *quick, left_over = fast_call(*args)
    return lax.cond(left_over[0] > 0.5, lambda: tuple(full_call(*args)), lambda: tuple(quick))


def solution(mesh):
    placed = (
        P(("group", "cluster"), None),
        P(("group", "cluster"), None),
        P(("group", "cluster"), None),
        P(("group", "cluster")),
        P(("group", "cluster"), None),
        P("cluster", None),
        P(),
    )
    return jax.shard_map(
        per_device,
        mesh=mesh,
        in_specs=placed,
        out_specs=(
            P(("group", "cluster"), None),
            P(("group", "cluster"), None),
            P("cluster", None),
            P(),
            P(),
        ),
        check_vma=False,
    )
```
